256 devices in a mesh: gx: 32 (over z, y), dp: 8 (over x, core).
Axes of the slice: x: 4, y: 4, z: 8, core: 2. Of those that a mesh axis runs over, the one named last changes fastest.
Arguments:
- inputs: bfloat16 [8, 128, 64, 32, 128], P('dp', 'gx'), may hold values from -6 to 6
- spectral_weights: bfloat16 [32, 2, 32, 32, 256], P('gx'), may hold values from -0.75 to 0.75
- skip_weights: bfloat16 [32, 32], replicated, may hold values from -1 to 1
- cotangent: bfloat16 [8, 128, 64, 32, 128], P('dp', 'gx'), may hold values from -6 to 6
Outputs:
- outputs: bfloat16 [8, 128, 64, 32, 128], P('dp', 'gx')
- grad_inputs: bfloat16 [8, 128, 64, 32, 128], P('dp', 'gx')
- weight_grad: float32 [32, 2, 32, 32, 256], P('gx', None, 'dp')
The draws below stay inside these ranges and needn't reach their ends.
All inputs are finite; a program needn't handle non-finite values.
Results may differ from the reference program's by a relative error of at most 0.04.
Values may be sent and summed in bfloat16 or wider, within the bound.
A program may use at most 128 MiB of HBM per device.

```python
import math
import jax
import jax.numpy as jnp
from jax import lax

C = 32
MX = 32
MY = 16
MZ = 16
NY = 64
NZ = 128
NX = 128
SAMPLES = 8


def level_of(key, dims, pieces, least, top_value):
    loudness, own = 1.0, jax.random.fold_in(key, 6)
    for axis_at, shards_of in pieces:
        heights = jnp.exp(jax.random.uniform(jax.random.fold_in(own, axis_at), (shards_of,), jnp.float32, least / len(pieces), top_value / len(pieces)))
        loudness = loudness * jnp.repeat(heights, dims[axis_at] // shards_of).reshape([-1 if axis == axis_at else 1 for axis in range(len(dims))])
    return loudness


def noise(key, shape, spread, bound, split=(), kind=jnp.bfloat16):
    gain = level_of(key, shape, split, -0.22, 0.18) if split else 1.0
    values = jax.random.normal(key, shape, jnp.float32) * spread * gain
    return jnp.minimum(jnp.maximum(values, -bound), bound).astype(kind)


def setup_inputs(seed: int = 0) -> dict:
    key_list = jax.random.split(jax.random.key(seed), 5)
    return {
        "inputs": noise(key_list[0], (SAMPLES, NX, NY, C, NZ), 1.0, 6.0, ((0, 8), (1, 32))),
        "spectral_weights": noise(key_list[1], (MX, 2, C, C, MY * MZ), (2 * C) ** -0.5, 0.75, ((0, 32),)),
        "skip_weights": noise(key_list[2], (C, C), C ** -0.5, 1.0),
        "cotangent": noise(key_list[3], (SAMPLES, NX, NY, C, NZ), 1.0, 6.0, ((0, 8), (1, 32))),
    }


def signed_of(indices, count):
    return jnp.where(indices < count // 2, indices, indices - count)

def twiddle(positions, freqs, length):
    phase = positions[:, None] * freqs[None, :] % length
    angle = 2.0 * math.pi / length * phase.astype(jnp.float32)
    return (jnp.cos(angle), jnp.sin(angle))

def rotation(tables, sign_factor):
    cos_table, sin_table = tables
    upper = jnp.stack([cos_table, sign_factor * sin_table])
    lower = jnp.stack([-sign_factor * sin_table, cos_table])
    return jnp.stack([upper, lower]).astype(jnp.bfloat16)

def fdot(form, left, right):
    return jnp.einsum(form, left.astype(jnp.float32), right.astype(jnp.float32), precision=lax.Precision.HIGHEST)

def forward_planes(field, y_table, z_rotation):
    batch_size, slab_rows, grid_y, channels, grid_z = field.shape
    modes_y = y_table.shape[1] // 2
    modes_z = z_rotation.shape[3]
    along_y = fdot('nxycz,yk->nxckz', field, y_table).astype(jnp.bfloat16)
    along_y = along_y.reshape(batch_size, slab_rows, channels, 2, modes_y, grid_z)
    planes = fdot('nxcayz,abzk->xnbcyk', along_y, z_rotation).astype(jnp.bfloat16)
    return planes.reshape(slab_rows, batch_size, 2, channels, modes_y * modes_z)

def inverse_planes(spectral, z_rotation, y_inverse):
    slab_rows, batch_size, parts, channels, modes = spectral.shape
    modes_y = y_inverse.shape[1]
    shaped = spectral.reshape(slab_rows, batch_size, 2, channels, modes_y, modes // modes_y)
    along_z = fdot('xnacyk,abzk->nxcbyz', shaped, z_rotation).astype(jnp.bfloat16)
    return fdot('nxcbyz,byw->nxwcz', along_z, y_inverse)

def complex_mix(modes_arr, weights):

    def product(left, right):
        return fdot('knim,kiom->knom', left, right)
    real_part = product(modes_arr[:, :, 0], weights[:, 0]) - product(modes_arr[:, :, 1], weights[:, 1])
    imag_part = product(modes_arr[:, :, 0], weights[:, 1]) + product(modes_arr[:, :, 1], weights[:, 0])
    return jnp.stack([real_part, imag_part], axis=2)

def conj_mix(back, weights):

    def product(left, right):
        return fdot('knom,kiom->knim', left, right)
    real_part = product(back[:, :, 0], weights[:, 0]) + product(back[:, :, 1], weights[:, 1])
    imag_part = product(back[:, :, 1], weights[:, 0]) - product(back[:, :, 0], weights[:, 1])
    return jnp.stack([real_part, imag_part], axis=2)

def weight_terms(modes_arr, back):

    def outer(left, right):
        return fdot('knim,knom->kiom', left, right)
    real_part = outer(modes_arr[:, :, 0], back[:, :, 0]) + outer(modes_arr[:, :, 1], back[:, :, 1])
    imag_part = outer(modes_arr[:, :, 0], back[:, :, 1]) - outer(modes_arr[:, :, 1], back[:, :, 0])
    return jnp.stack([real_part, imag_part], axis=1)

def reference(inputs, spectral_weights, skip_weights, cotangent):
    y_pair = twiddle(jnp.arange(NY, dtype=jnp.int32), signed_of(jnp.arange(MY, dtype=jnp.int32), MY), NY)
    y_table = jnp.concatenate([y_pair[0], -y_pair[1]], axis=1).astype(jnp.bfloat16)
    y_inverse = jnp.stack([y_pair[0].T, -y_pair[1].T]).astype(jnp.bfloat16)
    z_pair = twiddle(jnp.arange(NZ, dtype=jnp.int32), jnp.arange(MZ, dtype=jnp.int32), NZ)
    z_forward = rotation(z_pair, -1.0)
    z_backward = rotation(z_pair, 1.0)
    x_pair = twiddle(jnp.arange(NX, dtype=jnp.int32), signed_of(jnp.arange(MX, dtype=jnp.int32), MX), NX)
    x_forward = rotation(x_pair, -1.0)
    x_backward = rotation(x_pair, 1.0)
    grid_scale = 1.0 / math.sqrt(NX * NY * NZ)
    mode_scale = 1.0 / math.sqrt(MX * MY * MZ)

    def single(pair):
        sample, grad_out = pair
        sample = sample[None]
        grad_out = grad_out[None]
        planes = forward_planes(sample, y_table, z_forward)
        modes_arr = (fdot('xnacm,abxk->knbcm', planes, x_forward) * grid_scale).astype(jnp.bfloat16)
        mixed = complex_mix(modes_arr, spectral_weights).astype(jnp.bfloat16)
        slab = fdot('knacm,abxk->xnbcm', mixed, x_backward).astype(jnp.bfloat16)
        pre = inverse_planes(slab, z_backward, y_inverse) * mode_scale + fdot('nxycz,cd->nxydz', sample, skip_weights)
        activated, pullback = jax.vjp(jax.nn.gelu, pre)
        gpre = pullback(grad_out.astype(jnp.float32))[0].astype(jnp.bfloat16)
        gplanes = forward_planes(gpre, y_table, z_forward)
        back = (fdot('xnacm,abxk->knbcm', gplanes, x_forward) * mode_scale).astype(jnp.bfloat16)
        back_modes = conj_mix(back, spectral_weights).astype(jnp.bfloat16)
        terms = weight_terms(modes_arr, back)
        gslab = fdot('knacm,abxk->xnbcm', back_modes, x_backward).astype(jnp.bfloat16)
        grad_field = inverse_planes(gslab, z_backward, y_inverse) * grid_scale + fdot('nxydz,cd->nxycz', gpre, skip_weights)
        return (activated[0].astype(jnp.bfloat16), grad_field[0].astype(jnp.bfloat16), terms)
    outputs, grad_inputs, all_terms = lax.map(single, (inputs, cotangent))
    return (outputs, grad_inputs, lax.optimization_barrier(jnp.sum(all_terms, axis=0)))
```

```python
import functools
import math

import jax
import jax.numpy as jnp
import ml_dtypes
import numpy as np
from jax import lax
from jax.experimental import pallas as pl
from jax.experimental.pallas import tpu as pltpu
from jax.sharding import PartitionSpec as P

MESH = pl.DeviceIdType.MESH
F32 = jnp.float32
BF16 = jnp.bfloat16

NX, NY, NZ, MX, MY, MZ, C = 128, 64, 128, 32, 16, 16, 32
GX, DP = 32, 8
SLAB = NX // GX
GRID_SCALE = 1.0 / math.sqrt(NX * NY * NZ)
MODE_SCALE = 1.0 / math.sqrt(MX * MY * MZ)
PIECE = (GX, 16, 128)


def angles(length, freqs):
    phase = (np.arange(length)[:, None] * freqs[None, :]) % length
    angle = np.float32(2.0 * math.pi / length) * phase.astype(np.float32)
    return np.cos(angle).astype(np.float32), np.sin(angle).astype(np.float32)


def signed(count):
    k = np.arange(count)
    return np.where(k < count // 2, k, k - count)


def tables():
    bf = ml_dtypes.bfloat16
    cz, sz = angles(NZ, np.arange(MZ))
    zt = np.zeros((MZ, 2, 8, 8, NZ), np.float32)
    for q in range(8):
        zt[:, 0, q, q, :] = cz.T
        zt[:, 1, q, q, :] = -sz.T
    cy, sy = angles(NY, signed(MY))
    yb = np.stack([cy, -sy], axis=1)
    lt = np.einsum("ybk,cd->ycbkd", yb, np.eye(16, dtype=np.float32))
    cx, sx = angles(NX, signed(MX))
    rot = np.stack([np.stack([cx, sx]), np.stack([-sx, cx])])
    rot = rot.reshape(2, 2, GX, SLAB, MX)
    xf = np.einsum("pagrk,hj->phkgajr", rot, np.eye(2, dtype=np.float32))
    xf = xf.reshape(128, 512)
    return (
        zt.reshape(256, 1024).astype(bf),
        lt.reshape(1024, 512).astype(bf),
        xf.astype(bf),
        np.ascontiguousarray(xf.T).astype(bf),
    )


def dot(a, b):
    return jnp.dot(a, b, preferred_element_type=F32)


def dot_nt(a, b):
    return lax.dot_general(a, b, (((1,), (1,)), ((), ())), preferred_element_type=F32)


def iota(shape, axis):
    return lax.broadcasted_iota(jnp.int32, shape, axis)


def swap16(x):
    _, rows, _ = x.shape
    for s in (1, 2, 4, 8):
        keep_low = (iota((rows, 128), 1) & s) == 0
        parts = [None] * 16
        for i in range(16):
            if i & s:
                continue
            low, high = x[i], x[i + s]
            parts[i] = jnp.where(keep_low, low, pltpu.roll(high, s, 1))
            parts[i + s] = jnp.where(keep_low, pltpu.roll(low, 128 - s, 1), high)
        x = parts if s == 8 else _Stack(parts, rows)
    return x


class _Stack:
    def __init__(self, parts, rows):
        self.parts, self.shape = parts, (16, rows, 128)

    def __getitem__(self, i):
        return self.parts[i]


def gelu_pair(x):
    k0 = math.sqrt(2.0 / math.pi)
    x2 = x * x
    t = jnp.tanh(k0 * (x + 0.044715 * (x2 * x)))
    half = 0.5 * (1.0 + t)
    slope = half + (0.5 * k0) * x * (1.0 - t * t) * (1.0 + (3.0 * 0.044715) * x2)
    return x * half, slope


def kernel(
    x_hbm, w_hbm, s_ref, ct_hbm, zt_hbm, lt_hbm, xf_hbm, xi_hbm,
    out_hbm, gin_hbm, wg_hbm,
    f_v, ct_v, o_v, gp_v, zt_v, lt_v, xf_v, xi_v, wl_v,
    sw, sa1, sd1, sa2, sd2, swg,
    ra1, rd1, ra2, rd2, rwg,
    wall, mall, ball,
    m_v, p_v, q_v, gx_v, e_v, wt_v, wo_v, ks_v, kb_v,
    lsem, ss, rs,
):
    me = lax.axis_index("gx")
    d = lax.axis_index("dp")
    bar = pltpu.get_barrier_semaphore()

    def greet_g(p, c):
        pl.semaphore_signal(bar, inc=1, device_id={"gx": lax.rem(me + p, GX)}, device_id_type=MESH)
        return c

    def greet_d(p, c):
        pl.semaphore_signal(bar, inc=1, device_id={"dp": lax.rem(d + p, DP)}, device_id_type=MESH)
        return c

    part, ih0, oh0 = d // 4, lax.rem(d // 2, 2), lax.rem(d, 2)
    w_copy = pltpu.make_async_copy(
        w_hbm.at[part, pl.ds(ih0 * 16, 16), pl.ds(oh0 * 16, 16), :], wl_v, lsem.at[0]
    )
    w_copy.start()
    zt_copy = pltpu.make_async_copy(zt_hbm, zt_v, lsem.at[1])
    zt_copy.start()
    f_copy = pltpu.make_async_copy(x_hbm, f_v, lsem.at[2])
    f_copy.start()
    lt_copy = pltpu.make_async_copy(lt_hbm, lt_v, lsem.at[3])
    lt_copy.start()
    xf_copy = pltpu.make_async_copy(xf_hbm, xf_v, lsem.at[4])
    xf_copy.start()
    xi_copy = pltpu.make_async_copy(xi_hbm, xi_v, lsem.at[5])
    xi_copy.start()
    ct_copy = pltpu.make_async_copy(ct_hbm, ct_v, lsem.at[6])
    ct_copy.start()
    lax.fori_loop(1, GX, greet_g, 0)
    lax.fori_loop(1, DP, greet_d, 0)

    def spread(send, recv, n):
        def body(p, c):
            t = lax.rem(me + p, GX)
            pltpu.make_async_remote_copy(
                send.at[t], recv.at[me], ss.at[n], rs.at[n],
                device_id={"gx": t}, device_id_type=MESH,
            ).start()
            return c

        lax.fori_loop(1, GX, body, 0)
        recv[me] = send[me]

    def wait_bytes(ref, sem, count):
        view = ref.at[pl.ds(0, count)]
        pltpu.make_async_copy(view, view, sem).wait()

    def share(buf, n):
        def body(p, c):
            pltpu.make_async_remote_copy(
                buf.at[d], buf.at[d], ss.at[n], rs.at[n],
                device_id={"dp": lax.rem(d + p, DP)}, device_id_type=MESH,
            ).start()
            return c

        lax.fori_loop(1, DP, body, 0)

    w_copy.wait()
    for kyh in range(2):
        wv = wl_v[:, :, kyh * 128:(kyh + 1) * 128].astype(F32)
        swapped = swap16(wv)
        for kz in range(16):
            sw[kyh * 16 + kz] = swapped[kz].astype(BF16)

    def planes(field, send):
        def body(t, acc):
            blocks = [
                field[x, pl.ds(t * 16, 16), h].reshape(256, 128)
                for h in range(2) for x in range(SLAB)
            ]
            fc = jnp.concatenate(blocks, axis=1)
            along_z = dot_nt(zt_v[...], fc).astype(BF16)
            return acc + dot(along_z, lt_v[pl.ds(pl.multiple_of(t * 256, 256), 256), :])

        u = lax.fori_loop(0, 4, body, jnp.zeros((256, 512), F32))
        u = u.reshape(16, 2, 8, 512)
        u0, u1 = u[:, 0], u[:, 1]
        re = u0[:, :, :256] - u1[:, :, 256:]
        im = u0[:, :, 256:] + u1[:, :, :256]
        both = jnp.stack([re, im], axis=1).reshape(16, 16, 256).astype(BF16)
        send[0:16] = both[:, :, :128]
        send[16:32] = both[:, :, 128:]

    zt_copy.wait()
    lt_copy.wait()
    f_copy.wait()
    planes(f_v, sa1)

    pl.semaphore_wait(bar, GX - 1 + DP - 1)

    def body_w(p, c):
        t = lax.rem(me + p, GX)
        pltpu.make_async_remote_copy(
            sw.at[t], wall.at[d, me], ss.at[0], rs.at[0],
            device_id={"gx": t}, device_id_type=MESH,
        ).start()
        return c

    lax.fori_loop(1, GX, body_w, 0)
    wall[d, me] = sw[me]
    spread(sa1, ra1, 1)

    er = iota((256, 32), 0)
    expand = (lax.rem(er, 32) == iota((256, 32), 1)).astype(F32).astype(BF16)
    same = iota((256, 256), 0) // 32 == iota((256, 256), 1) // 32
    sk = s_ref[...]
    es = dot(expand, sk).astype(BF16)
    kb_v[...] = jnp.where(same, dot_nt(es, expand), 0.0).astype(BF16)
    est = dot_nt(expand, sk).astype(BF16)
    ks_v[...] = jnp.where(same, dot_nt(est, expand), 0.0).astype(BF16)
    sum_l = (iota((64, 1024), 0) == iota((64, 1024), 1) // 16).astype(F32).astype(BF16)
    rep_l = (iota((1024, 64), 0) // 16 == iota((1024, 64), 1)).astype(F32).astype(BF16)
    ones_b = (iota((128, 128), 0) // 16 == iota((128, 128), 1) // 16).astype(F32).astype(BF16)
    diag = lax.rem(iota((1024, 128), 0), 16) == lax.rem(iota((1024, 128), 1), 16)

    wait_bytes(sw, rs.at[0], GX - 1)

    mate = d + 1 - 2 * lax.rem(d, 2)

    def body_x(p, c):
        pltpu.make_async_remote_copy(
            wall.at[d], wall.at[d], ss.at[2], rs.at[2],
            device_id={"dp": lax.rem(d + 2 * p, DP)}, device_id_type=MESH,
        ).start()
        return c

    lax.fori_loop(1, 4, body_x, 0)

    def body_c(p, c):
        slot = lax.rem(d + 2 * p, DP)
        pltpu.make_async_remote_copy(
            wall.at[slot], wall.at[slot], ss.at[3], rs.at[3],
            device_id={"dp": mate}, device_id_type=MESH,
        ).start()
        return c

    body_c(0, 0)

    def to_modes(recv, scale):
        r = recv[...].reshape(512, 128)
        return (dot(xf_v[...], r) * scale).astype(BF16)

    def to_slabs(mixed, send):
        send[...] = dot(xi_v[...], mixed).astype(BF16).reshape(PIECE)

    xf_copy.wait()
    xi_copy.wait()
    wait_bytes(ra1, rs.at[1], GX - 1)
    modes = to_modes(ra1, GRID_SCALE)
    mall[d] = modes
    share(mall, 4)
    m_v[...] = modes.astype(F32)

    wait_bytes(wall, rs.at[2], 3)
    lax.fori_loop(1, 4, body_c, 0)
    wait_bytes(wall, rs.at[3], 4)

    def weight(a, h, oh, k):
        return wall[4 * a + 2 * h + oh, k].astype(F32)

    def mix(k, c):
        mr = [m_v[pl.ds(h * 32 + k, 1), :] for h in range(2)]
        mi = [m_v[pl.ds(64 + h * 32 + k, 1), :] for h in range(2)]
        for oh in range(2):
            re = im = None
            for h in range(2):
                wr, wi = weight(0, h, oh, k), weight(1, h, oh, k)
                r = wr * mr[h] - wi * mi[h]
                i = wr * mi[h] + wi * mr[h]
                re = r if re is None else re + r
                im = i if im is None else im + i
            row = pl.multiple_of(oh * 512 + k * 16, 16)
            p_v[0, pl.ds(row, 16), :] = re.astype(BF16)
            p_v[1, pl.ds(row, 16), :] = im.astype(BF16)
        return c

    lax.fori_loop(0, MX, mix, 0)
    mixed = []
    for a in range(2):
        q = jnp.where(diag, dot(p_v[a], ones_b), 0.0).astype(BF16)
        mixed.append(dot(sum_l, q))
    to_slabs(jnp.concatenate(mixed, axis=0).astype(BF16), sd1)
    spread(sd1, rd1, 5)

    def unpack(recv):
        g = recv[...].astype(F32)
        g = jnp.concatenate([g[:16], g[16:]], axis=2).reshape(16, 2, 8, 256)
        turned = jnp.stack([g[:, 1], -g[:, 0]], axis=1).reshape(256, 256)
        gx_v[:, 0:256] = g.reshape(256, 256).astype(BF16)
        gx_v[:, 256:512] = turned.astype(BF16)

    def fields(scale, source, channel_map, emit):
        def body(t, c):
            lt_c = lt_v[pl.ds(pl.multiple_of(t * 128, 128), 128), :]
            vt = (dot_nt(lt_c, gx_v[...]) * scale).astype(BF16)
            for x in range(0, SLAB, 2):
                src = jnp.concatenate(
                    [source[x + i, pl.ds(t * 8, 8)].reshape(256, 128) for i in range(2)], axis=1
                )
                skip = dot(channel_map[...], src).reshape(8, 2, 16, 256)
                for h in range(2):
                    lo = (h * 4 + x) * 128
                    fld = dot(vt, zt_v[:, lo:lo + 256]).reshape(8, 16, 256)
                    total = fld + skip[:, h]
                    for i in range(2):
                        emit(x + i, t, h, total[:, :, i * 128:(i + 1) * 128])
            return c

        lax.fori_loop(0, 8, body, 0)

    ct_copy.wait()
    wait_bytes(rd1, rs.at[5], GX - 1)
    unpack(rd1)

    def emit_forward(x, t, h, pre):
        act, slope = gelu_pair(pre)
        ct = ct_v[x, pl.ds(t * 8, 8), h].astype(F32)
        o_v[x, pl.ds(t * 8, 8), h] = act.astype(BF16)
        gp_v[x, pl.ds(t * 8, 8), h] = (ct * slope).astype(BF16)

    fields(MODE_SCALE, f_v, ks_v, emit_forward)
    o_copy = pltpu.make_async_copy(o_v, out_hbm, lsem.at[7])
    o_copy.start()

    planes(gp_v, sa2)
    spread(sa2, ra2, 6)
    wait_bytes(ra2, rs.at[6], GX - 1)
    back = to_modes(ra2, MODE_SCALE)
    ball[d] = back
    share(ball, 7)

    for a in range(2):
        rows = jnp.where(diag, dot(rep_l, back[64 * a:64 * a + 64]), 0.0).astype(BF16)
        q_v[a] = dot(rows, ones_b)

    def conj_mix(k, c):
        for h in range(2):
            re = im = None
            for oh in range(2):
                row = pl.multiple_of(oh * 512 + k * 16, 16)
                br, bi = q_v[0, pl.ds(row, 16), :], q_v[1, pl.ds(row, 16), :]
                wr, wi = weight(0, h, oh, k), weight(1, h, oh, k)
                r = wr * br + wi * bi
                i = wr * bi - wi * br
                re = r if re is None else re + r
                im = i if im is None else im + i
            row = pl.multiple_of(h * 512 + k * 16, 16)
            p_v[0, pl.ds(row, 16), :] = re.astype(BF16)
            p_v[1, pl.ds(row, 16), :] = im.astype(BF16)
        return c

    lax.fori_loop(0, MX, conj_mix, 0)
    back_modes = [dot(sum_l, p_v[a]) for a in range(2)]
    to_slabs(jnp.concatenate(back_modes, axis=0).astype(BF16), sd2)
    spread(sd2, rd2, 8)

    wait_bytes(mall, rs.at[4], DP - 1)
    sel_r, sel_c = iota((128, 512), 0), iota((128, 512), 1)
    chan = 4 * lax.rem(d, 4) + sel_c // 128
    pick = (lax.rem(sel_r, 16) == chan) & (sel_r // 16 == lax.rem(sel_c, 128) // 16)
    pick = pick.astype(F32).astype(BF16)
    ihd = d // 4
    for a in range(2):
        start = pl.multiple_of(a * 64 + ihd * 32, 32)
        rows = mall[:, pl.ds(start, 32), :].reshape(256, 128)
        e_v[a] = dot(rows, pick)
    wait_bytes(ball, rs.at[7], DP - 1)
    for oh in range(2):
        for i4 in range(4):
            def add(n, acc):
                re, im = acc
                row = pl.multiple_of(n * 32, 32)
                er_ = e_v[0, pl.ds(row, 32), i4 * 128:(i4 + 1) * 128]
                ei_ = e_v[1, pl.ds(row, 32), i4 * 128:(i4 + 1) * 128]
                br = ball[n, oh * 32:oh * 32 + 32, :].astype(F32)
                bi = ball[n, 64 + oh * 32:64 + oh * 32 + 32, :].astype(F32)
                return re + er_ * br + ei_ * bi, im + er_ * bi - ei_ * br

            zero = jnp.zeros((32, 128), F32)
            re, im = lax.fori_loop(0, DP, add, (zero, zero))
            wt_v[:, i4 * 2 + oh, :] = re
            wt_v[:, 8 + i4 * 2 + oh, :] = im
    swg[...] = wt_v[...].astype(BF16)
    spread(swg, rwg, 9)

    wait_bytes(rd2, rs.at[8], GX - 1)
    unpack(rd2)
    o_copy.wait()

    def emit_backward(x, t, h, total):
        o_v[x, pl.ds(t * 8, 8), h] = total.astype(BF16)

    fields(GRID_SCALE, gp_v, kb_v, emit_backward)
    g_copy = pltpu.make_async_copy(o_v, gin_hbm, lsem.at[8])
    g_copy.start()

    wait_bytes(rwg, rs.at[9], GX - 1)
    for kyh in range(2):
        swapped = swap16(rwg[kyh * 16:kyh * 16 + 16].astype(F32))
        for o in range(16):
            wo_v[:, o, kyh * 128:(kyh + 1) * 128] = swapped[o]
    wg_copy = pltpu.make_async_copy(wo_v, wg_hbm, lsem.at[9])
    wg_copy.start()

    for n in (0, 1, 5, 6, 8, 9):
        wait_bytes(ra1, ss.at[n], GX - 1)
    wait_bytes(wall, ss.at[2], 3)
    wait_bytes(wall, ss.at[3], 4)
    wait_bytes(mall, ss.at[4], DP - 1)
    wait_bytes(ball, ss.at[7], DP - 1)
    g_copy.wait()
    wg_copy.wait()


def per_device(inputs, spectral_weights, skip_weights, cotangent, *tabs):
    shape5 = (SLAB, NY, 2, 16, NZ)
    any_spec = pl.BlockSpec(memory_space=pl.ANY)
    vm = pltpu.VMEM
    big = vm(shape5, BF16)
    piece = vm(PIECE, BF16)
    out, gin, wg = pl.pallas_call(
        kernel,
        out_shape=[
            jax.ShapeDtypeStruct(shape5, BF16),
            jax.ShapeDtypeStruct(shape5, BF16),
            jax.ShapeDtypeStruct((16, 16, 256), F32),
        ],
        in_specs=[any_spec, any_spec, pl.BlockSpec(memory_space=vm)] + [any_spec] * 5,
        out_specs=[any_spec] * 3,
        scratch_shapes=[
            big, big, big, big,
            vm((256, 1024), BF16), vm((1024, 512), BF16),
            vm((128, 512), BF16), vm((512, 128), BF16),
            vm((16, 16, 256), BF16),
            *([piece] * 11),
            vm((DP, *PIECE), BF16), vm((DP, 128, 128), BF16), vm((DP, 128, 128), BF16),
            vm((128, 128), F32), vm((2, 1024, 128), BF16), vm((2, 1024, 128), F32),
            vm((256, 512), BF16), vm((2, 256, 512), F32),
            vm(PIECE, F32), vm((16, 16, 256), F32),
            vm((256, 256), BF16), vm((256, 256), BF16),
            pltpu.SemaphoreType.DMA((10,)),
            pltpu.SemaphoreType.DMA((10,)),
            pltpu.SemaphoreType.DMA((10,)),
        ],
        compiler_params=pltpu.CompilerParams(
            collective_id=0, has_side_effects=True, vmem_limit_bytes=48 * 1024 * 1024
        ),
        cost_estimate=pl.CostEstimate(flops=8_000_000_000, bytes_accessed=12_000_000, transcendentals=1_048_576),
        name="spectral_layer",
    )(
        inputs.reshape(shape5), spectral_weights[0], skip_weights,
        cotangent.reshape(shape5), *tabs,
    )
    return (
        out.reshape(inputs.shape),
        gin.reshape(inputs.shape),
        wg.reshape(1, 2, 4, C, MY * MZ),
    )


def solution(mesh):
    field_spec = P("dp", "gx", None, None, None)
    in_specs = (field_spec, P("gx", None, None, None, None), P(), field_spec) + (P(),) * 4
    out_specs = (field_spec, field_spec, P("gx", None, "dp", None, None))
    mapped = jax.shard_map(
        per_device, mesh=mesh, in_specs=in_specs, out_specs=out_specs, check_vma=False
    )
    tabs = tables()

    def run(inputs, spectral_weights, skip_weights, cotangent):
        return mapped(
            inputs, spectral_weights, skip_weights, cotangent, *[jnp.asarray(t) for t in tabs]
        )

    return run
```

```python
import functools
import math

import jax
import jax.numpy as jnp
import ml_dtypes
import numpy as np
from jax import lax
from jax.experimental import pallas as pl
from jax.experimental.pallas import tpu as pltpu
from jax.sharding import PartitionSpec as P

MESH = pl.DeviceIdType.MESH
F32 = jnp.float32
BF16 = jnp.bfloat16

NX, NY, NZ, MX, MY, MZ, C = 128, 64, 128, 32, 16, 16, 32
GX, DP = 32, 8
SLAB = NX // GX
GRID_SCALE = 1.0 / math.sqrt(NX * NY * NZ)
MODE_SCALE = 1.0 / math.sqrt(MX * MY * MZ)
PIECE = (GX, 16, 128)
ROUNDS = (3, 2, 1, 0)


def angles(length, freqs):
    phase = (np.arange(length)[:, None] * freqs[None, :]) % length
    angle = np.float32(2.0 * math.pi / length) * phase.astype(np.float32)
    return np.cos(angle).astype(np.float32), np.sin(angle).astype(np.float32)


def signed(count):
    k = np.arange(count)
    return np.where(k < count // 2, k, k - count)


def tables():
    bf = ml_dtypes.bfloat16
    cz, sz = angles(NZ, np.arange(MZ))
    zt = np.zeros((MZ, 2, 8, 8, NZ), np.float32)
    for q in range(8):
        zt[:, 0, q, q, :] = cz.T
        zt[:, 1, q, q, :] = -sz.T
    cy, sy = angles(NY, signed(MY))
    yb = np.stack([cy, -sy], axis=1)
    lt = np.einsum("ybk,cd->ycbkd", yb, np.eye(16, dtype=np.float32))
    cx, sx = angles(NX, signed(MX))
    rot = np.stack([np.stack([cx, sx]), np.stack([-sx, cx])])
    rot = rot.reshape(2, 2, GX, SLAB, MX)
    xf = np.einsum("pagrk,hj->phkgajr", rot, np.eye(2, dtype=np.float32))
    xf = xf.reshape(128, 512)
    return (
        zt.reshape(256, 1024).astype(bf),
        np.ascontiguousarray(zt.reshape(256, 1024).T).astype(bf),
        lt.reshape(1024, 512).astype(bf),
        xf.astype(bf),
        np.ascontiguousarray(xf.T).astype(bf),
    )


def dot(a, b):
    return jnp.dot(a, b, preferred_element_type=F32)


def dot_nt(a, b):
    return lax.dot_general(a, b, (((1,), (1,)), ((), ())), preferred_element_type=F32)


def iota(shape, axis):
    return lax.broadcasted_iota(jnp.int32, shape, axis)


def swap16(x):
    _, rows, _ = x.shape
    for s in (1, 2, 4, 8):
        keep_low = (iota((rows, 128), 1) & s) == 0
        parts = [None] * 16
        for i in range(16):
            if i & s:
                continue
            low, high = x[i], x[i + s]
            parts[i] = jnp.where(keep_low, low, pltpu.roll(high, s, 1))
            parts[i + s] = jnp.where(keep_low, pltpu.roll(low, 128 - s, 1), high)
        x = parts if s == 8 else _Stack(parts, rows)
    return x


class _Stack:
    def __init__(self, parts, rows):
        self.parts, self.shape = parts, (16, rows, 128)

    def __getitem__(self, i):
        return self.parts[i]


def gelu_pair(x):
    k0 = math.sqrt(2.0 / math.pi)
    x2 = x * x
    t = jnp.tanh(k0 * (x + 0.044715 * (x2 * x)))
    half = 0.5 * (1.0 + t)
    slope = half + (0.5 * k0) * x * (1.0 - t * t) * (1.0 + (3.0 * 0.044715) * x2)
    return x * half, slope


def kernel(
    x_hbm, w_hbm, s_ref, ct_hbm, zt_hbm, zf_hbm, lt_hbm, xf_hbm, xi_hbm,
    out_hbm, gin_hbm, wg_hbm,
    f_v, ct_v, o_v, gp_v, zt_v, zf_v, lt_v, xf_v, xi_v, wl_v,
    sw, sa1, sd1, sa2, sd2, swg,
    ra1, rd1, ra2, rd2, rwg,
    wall, mall, ball,
    m_v, p_v, q_v, gx_v, e_v, sk_v, wt_v, wo_v, ks_v, kb_v,
    lsem, ss, rs,
):
    me = lax.axis_index("gx")
    d = lax.axis_index("dp")
    bar = pltpu.get_barrier_semaphore()

    def peer(q):
        i, j = q // 4, lax.rem(q, 4)
        dz = 4 + (1 - 2 * lax.rem(i, 2)) * ((i + 1) // 2)
        dy = 2 + (1 - 2 * lax.rem(j, 2)) * ((j + 1) // 2)
        return lax.rem(me // 4 + dz, 8) * 4 + lax.rem(lax.rem(me, 4) + dy, 4)

    def greet_g(q, c):
        pl.semaphore_signal(bar, inc=1, device_id={"gx": peer(q)}, device_id_type=MESH)
        return c

    def greet_d(p, c):
        pl.semaphore_signal(bar, inc=1, device_id={"dp": lax.rem(d + p, DP)}, device_id_type=MESH)
        return c

    lax.fori_loop(0, GX - 1, greet_g, 0, unroll=True)
    lax.fori_loop(1, DP, greet_d, 0, unroll=True)

    pending = {}

    def load(name, src, dst, n):
        copy = pltpu.make_async_copy(src, dst, lsem.at[n])
        copy.start()
        pending[name] = copy.wait

    def settle(*names):
        for name in names:
            pending.pop(name)()

    def wait_bytes(ref, sem, count):
        view = ref.at[pl.ds(0, count)]
        pltpu.make_async_copy(view, view, sem).wait()

    def expect(name, n, ref, count):
        pending[name] = lambda: wait_bytes(ref, rs.at[n], count)
        pending[name + "_sent"] = lambda: wait_bytes(ref, ss.at[n], count)

    part, ih0, oh0 = d // 4, lax.rem(d // 2, 2), lax.rem(d, 2)
    w_mine = w_hbm.at[part, pl.ds(ih0 * 16, 16), pl.ds(oh0 * 16, 16), :]
    load("w", w_mine, wl_v, 0)
    load("zf", zf_hbm, zf_v, 1)
    load("f", x_hbm, f_v, 2)
    load("lt", lt_hbm, lt_v, 3)
    load("xf", xf_hbm, xf_v, 4)
    load("xi", xi_hbm, xi_v, 5)
    load("zt", zt_hbm, zt_v, 10)
    load("ct", ct_hbm, ct_v, 6)

    def spread(name, send, recv, n):
        def body(q, c):
            t = peer(q)
            pltpu.make_async_remote_copy(
                send.at[t], recv.at[me], ss.at[n], rs.at[n],
                device_id={"gx": t}, device_id_type=MESH,
            ).start()
            return c

        lax.fori_loop(0, GX - 1, body, 0, unroll=True)
        recv[me] = send[me]
        expect(name, n, recv, GX - 1)

    def share(name, buf, n):
        def body(p, c):
            pltpu.make_async_remote_copy(
                buf.at[d], buf.at[d], ss.at[n], rs.at[n],
                device_id={"dp": lax.rem(d + p, DP)}, device_id_type=MESH,
            ).start()
            return c

        for p in (4, 5, 3, 6, 2, 7, 1):
            body(p, 0)
        expect(name, n, buf, DP - 1)

    settle("w")
    for kyh in range(2):
        wv = wl_v[:, :, kyh * 128:(kyh + 1) * 128].astype(F32)
        swapped = swap16(wv)
        for kz in range(16):
            sw[kyh * 16 + kz] = swapped[kz].astype(BF16)

    def planes(field, send):
        def body(t, acc):
            blocks = [
                field[x, pl.ds(t * 16, 16), h].reshape(256, 128)
                for h in range(2) for x in range(SLAB)
            ]
            fc = jnp.concatenate(blocks, axis=1)
            along_z = dot(fc, zf_v[...]).T.astype(BF16)
            return acc + dot(along_z, lt_v[pl.ds(pl.multiple_of(t * 256, 256), 256), :])

        u = lax.fori_loop(0, 4, body, jnp.zeros((256, 512), F32))
        u = u.reshape(16, 2, 8, 512)
        u0, u1 = u[:, 0], u[:, 1]
        re = u0[:, :, :256] - u1[:, :, 256:]
        im = u0[:, :, 256:] + u1[:, :, :256]
        both = jnp.stack([re, im], axis=1).reshape(16, 16, 256).astype(BF16)
        send[0:16] = both[:, :, :128]
        send[16:32] = both[:, :, 128:]

    pl.semaphore_wait(bar, GX - 1 + DP - 1)

    def body_w(q, c):
        t = peer(q)
        pltpu.make_async_remote_copy(
            sw.at[t], wall.at[d, me], ss.at[0], rs.at[20 + q // 8],
            device_id={"gx": t}, device_id_type=MESH,
        ).start()
        return c

    for r in ROUNDS:
        lax.fori_loop(8 * r, min(8 * r + 8, GX - 1), body_w, 0, unroll=True)
    wall[d, me] = sw[me]
    pending["weights_sent"] = lambda: wait_bytes(sw, ss.at[0], GX - 1)
    for r in ROUNDS:
        pending[f"weights_gx{r}"] = lambda r=r: wait_bytes(sw, rs.at[20 + r], min(8, GX - 1 - 8 * r))
    settle("zf", "lt", "f")
    planes(f_v, sa1)


    spread("a1", sa1, ra1, 1)

    er = iota((256, 32), 0)
    expand = (lax.rem(er, 32) == iota((256, 32), 1)).astype(F32).astype(BF16)
    same = iota((256, 256), 0) // 32 == iota((256, 256), 1) // 32
    sk = s_ref[...]
    es = dot(expand, sk).astype(BF16)
    kb_v[...] = jnp.where(same, dot_nt(es, expand), 0.0).astype(BF16)
    est = dot_nt(expand, sk).astype(BF16)
    ks_v[...] = jnp.where(same, dot_nt(est, expand), 0.0).astype(BF16)
    sum_l = (iota((64, 1024), 0) == iota((64, 1024), 1) // 16).astype(F32).astype(BF16)
    rep_l = (iota((1024, 64), 0) // 16 == iota((1024, 64), 1)).astype(F32).astype(BF16)
    ones_b = (iota((128, 128), 0) // 16 == iota((128, 128), 1) // 16).astype(F32).astype(BF16)
    diag = lax.rem(iota((1024, 128), 0), 16) == lax.rem(iota((1024, 128), 1), 16)

    mate = d + 1 - 2 * lax.rem(d, 2)

    def gather(slot, r, target, send_n, recv_n):
        for i in (2 * r, 2 * r + 1):
            dz = 4 + (1 - 2 * (i % 2)) * ((i + 1) // 2)
            z = lax.rem(me // 4 + 8 - dz, 8)
            block = wall.at[slot, pl.ds(4 * z, 4)]
            pltpu.make_async_remote_copy(
                block, block, ss.at[send_n], rs.at[recv_n],
                device_id={"dp": target}, device_id_type=MESH,
            ).start()

    for r in ROUNDS:
        settle(f"weights_gx{r}")
        for p in (2, 1, 3):
            gather(d, r, lax.rem(d + 2 * p, DP), 2, 24 + 3 * r + p - 1)
        gather(d, r, mate, 3, 3)

    def eight(sem):
        view = wall.at[0, pl.ds(0, 8)]
        pltpu.make_async_copy(view, view, sem).wait()

    for r in ROUNDS:
        for p in (1, 3, 2):
            pending[f"weights_x{r}{p}"] = lambda n=24 + 3 * r + p - 1: eight(rs.at[n])
    pending["weights_x_sent"] = lambda: wait_bytes(wall, ss.at[2], 3)

    def to_modes(recv, scale):
        r = recv[...].reshape(512, 128)
        return (dot(xf_v[...], r) * scale).astype(BF16)

    def to_slabs(mixed, send):
        send[...] = dot(xi_v[...], mixed).astype(BF16).reshape(PIECE)

    settle("xf", "xi", "a1")
    modes = to_modes(ra1, GRID_SCALE)
    mall[d] = modes
    m_v[...] = modes.astype(F32)

    for r in ROUNDS:
        for p in (1, 3, 2):
            settle(f"weights_x{r}{p}")
            gather(lax.rem(d + 8 - 2 * p, DP), r, mate, 3, 3)
    expect("weights_core", 3, wall, 4)
    settle("weights_core")

    def weight(a, h, oh, k):
        return wall[4 * a + 2 * h + oh, k].astype(F32)

    def mix(k, c):
        mr = [m_v[pl.ds(h * 32 + k, 1), :] for h in range(2)]
        mi = [m_v[pl.ds(64 + h * 32 + k, 1), :] for h in range(2)]
        for oh in range(2):
            re = im = None
            for h in range(2):
                wr, wi = weight(0, h, oh, k), weight(1, h, oh, k)
                r = wr * mr[h] - wi * mi[h]
                i = wr * mi[h] + wi * mr[h]
                re = r if re is None else re + r
                im = i if im is None else im + i
            row = pl.multiple_of(oh * 512 + k * 16, 16)
            p_v[0, pl.ds(row, 16), :] = re.astype(BF16)
            p_v[1, pl.ds(row, 16), :] = im.astype(BF16)
        return c

    lax.fori_loop(0, MX, mix, 0, unroll=4)
    mixed = []
    for a in range(2):
        q = jnp.where(diag, dot(p_v[a], ones_b), 0.0).astype(BF16)
        mixed.append(dot(sum_l, q))
    to_slabs(jnp.concatenate(mixed, axis=0).astype(BF16), sd1)
    spread("d1", sd1, rd1, 5)

    def unpack(recv):
        g = recv[...].astype(F32)
        g = jnp.concatenate([g[:16], g[16:]], axis=2).reshape(16, 2, 8, 256)
        turned = jnp.stack([g[:, 1], -g[:, 0]], axis=1).reshape(256, 256)
        gx_v[0:256, :] = g.reshape(256, 256).T.astype(BF16)
        gx_v[256:512, :] = turned.T.astype(BF16)

    def skips(source, channel_map):
        def body(t, c):
            for x in range(0, SLAB, 2):
                src = jnp.concatenate(
                    [source[x + i, pl.ds(t * 8, 8)].reshape(256, 128) for i in range(2)], axis=1
                )
                skip = dot(channel_map[...], src).reshape(8, 2, 16, 256)
                for i in range(2):
                    sk_v[x + i, pl.ds(t * 8, 8)] = skip[..., i * 128:(i + 1) * 128]
            return c

        lax.fori_loop(0, 8, body, 0)

    def fields(scale, emit):
        def body(t, c):
            lt_c = lt_v[pl.ds(pl.multiple_of(t * 128, 128), 128), :]
            vt = (dot(lt_c, gx_v[...]) * scale).astype(BF16)
            for x in range(0, SLAB, 2):
                for h in range(2):
                    lo = (h * 4 + x) * 128
                    fld = dot(vt, zt_v[:, lo:lo + 256]).reshape(8, 16, 256)
                    for i in range(2):
                        skip = sk_v[x + i, pl.ds(t * 8, 8), h]
                        emit(x + i, t, h, fld[:, :, i * 128:(i + 1) * 128] + skip)
            return c

        lax.fori_loop(0, 8, body, 0)

    share("mall", mall, 4)
    skips(f_v, ks_v)
    settle("ct", "zt", "d1")
    unpack(rd1)

    def emit_forward(x, t, h, pre):
        act, slope = gelu_pair(pre)
        ct = ct_v[x, pl.ds(t * 8, 8), h].astype(F32)
        o_v[x, pl.ds(t * 8, 8), h] = act.astype(BF16)
        gp_v[x, pl.ds(t * 8, 8), h] = (ct * slope).astype(BF16)

    fields(MODE_SCALE, emit_forward)
    load("out", o_v, out_hbm, 7)

    planes(gp_v, sa2)
    spread("a2", sa2, ra2, 6)
    skips(gp_v, kb_v)
    settle("a2")
    back = to_modes(ra2, MODE_SCALE)
    ball[d] = back
    share("ball", ball, 7)

    for a in range(2):
        rows = jnp.where(diag, dot(rep_l, back[64 * a:64 * a + 64]), 0.0).astype(BF16)
        q_v[a] = dot(rows, ones_b)

    def conj_mix(k, c):
        for h in range(2):
            re = im = None
            for oh in range(2):
                row = pl.multiple_of(oh * 512 + k * 16, 16)
                br, bi = q_v[0, pl.ds(row, 16), :], q_v[1, pl.ds(row, 16), :]
                wr, wi = weight(0, h, oh, k), weight(1, h, oh, k)
                r = wr * br + wi * bi
                i = wr * bi - wi * br
                re = r if re is None else re + r
                im = i if im is None else im + i
            row = pl.multiple_of(h * 512 + k * 16, 16)
            p_v[0, pl.ds(row, 16), :] = re.astype(BF16)
            p_v[1, pl.ds(row, 16), :] = im.astype(BF16)
        return c

    lax.fori_loop(0, MX, conj_mix, 0, unroll=4)
    back_modes = [dot(sum_l, p_v[a]) for a in range(2)]
    to_slabs(jnp.concatenate(back_modes, axis=0).astype(BF16), sd2)
    spread("d2", sd2, rd2, 8)

    settle("mall")
    sel_r, sel_c = iota((128, 512), 0), iota((128, 512), 1)
    chan = 4 * lax.rem(d, 4) + sel_c // 128
    pick = (lax.rem(sel_r, 16) == chan) & (sel_r // 16 == lax.rem(sel_c, 128) // 16)
    pick = pick.astype(F32).astype(BF16)
    ihd = d // 4
    for a in range(2):
        start = pl.multiple_of(a * 64 + ihd * 32, 32)
        rows = mall[:, pl.ds(start, 32), :].reshape(256, 128)
        e_v[a] = dot(rows, pick)
    settle("ball")
    for oh in range(2):
        for i4 in range(4):
            def add(n, acc):
                re, im = acc
                row = pl.multiple_of(n * 32, 32)
                er_ = e_v[0, pl.ds(row, 32), i4 * 128:(i4 + 1) * 128]
                ei_ = e_v[1, pl.ds(row, 32), i4 * 128:(i4 + 1) * 128]
                br = ball[n, oh * 32:oh * 32 + 32, :].astype(F32)
                bi = ball[n, 64 + oh * 32:64 + oh * 32 + 32, :].astype(F32)
                return re + er_ * br + ei_ * bi, im + er_ * bi - ei_ * br

            zero = jnp.zeros((32, 128), F32)
            re, im = lax.fori_loop(0, DP, add, (zero, zero))
            wt_v[:, i4 * 2 + oh, :] = re
            wt_v[:, 8 + i4 * 2 + oh, :] = im
    swg[...] = wt_v[...].astype(BF16)
    spread("wg", swg, rwg, 9)

    settle("d2", "out")
    unpack(rd2)

    def emit_backward(x, t, h, total):
        o_v[x, pl.ds(t * 8, 8), h] = total.astype(BF16)

    fields(GRID_SCALE, emit_backward)
    load("gin", o_v, gin_hbm, 8)

    settle("wg")
    for kyh in range(2):
        swapped = swap16(rwg[kyh * 16:kyh * 16 + 16].astype(F32))
        for o in range(16):
            wo_v[:, o, kyh * 128:(kyh + 1) * 128] = swapped[o]
    load("wg_out", wo_v, wg_hbm, 9)
    settle(*list(pending))


def writer(out_a, gin_a, wg_a, out_b, gin_b, wg_b, sem):
    pairs = [(a.at[i], b.at[i]) for a, b in ((out_a, out_b), (gin_a, gin_b)) for i in range(SLAB)]
    pairs.append((wg_a, wg_b))
    copies = [pltpu.make_async_copy(a, b, sem.at[n]) for n, (a, b) in enumerate(pairs)]
    for copy in copies:
        copy.start()
    for copy in copies:
        copy.wait()


def per_device(inputs, spectral_weights, skip_weights, cotangent, *tabs):
    shape5 = (SLAB, NY, 2, 16, NZ)
    any_spec = pl.BlockSpec(memory_space=pl.ANY)
    vm = pltpu.VMEM
    big = vm(shape5, BF16)
    piece = vm(PIECE, BF16)
    hbm = pl.BlockSpec(memory_space=pltpu.HBM)
    keep = functools.partial(pltpu.with_memory_space_constraint, memory_space=pltpu.HBM)
    shapes = [
        jax.ShapeDtypeStruct(shape5, BF16),
        jax.ShapeDtypeStruct(shape5, BF16),
        jax.ShapeDtypeStruct((16, 16, 256), F32),
    ]
    results = pl.pallas_call(
        kernel,
        out_shape=[vm(s.shape, s.dtype) for s in shapes],
        in_specs=[hbm, hbm, pl.BlockSpec(memory_space=vm)] + [hbm] * 6,
        out_specs=[any_spec] * 3,
        scratch_shapes=[
            big, big, big, big,
            vm((256, 1024), BF16), vm((1024, 256), BF16), vm((1024, 512), BF16),
            vm((128, 512), BF16), vm((512, 128), BF16),
            vm((16, 16, 256), BF16),
            *([piece] * 11),
            vm((DP, *PIECE), BF16), vm((DP, 128, 128), BF16), vm((DP, 128, 128), BF16),
            vm((128, 128), F32), vm((2, 1024, 128), BF16), vm((2, 1024, 128), F32),
            vm((512, 256), BF16), vm((2, 256, 512), F32), vm(shape5, F32),
            vm(PIECE, F32), vm((16, 16, 256), F32),
            vm((256, 256), BF16), vm((256, 256), BF16),
            pltpu.SemaphoreType.DMA((36,)),
            pltpu.SemaphoreType.DMA((36,)),
            pltpu.SemaphoreType.DMA((36,)),
        ],
        compiler_params=pltpu.CompilerParams(
            collective_id=0, has_side_effects=True, vmem_limit_bytes=40 * 1024 * 1024
        ),
        cost_estimate=pl.CostEstimate(flops=8_000_000_000, bytes_accessed=12_000_000, transcendentals=1_048_576),
        name="spectral_layer",
    )(
        keep(inputs.reshape(shape5)), keep(spectral_weights[0]), skip_weights,
        keep(cotangent.reshape(shape5)), *map(keep, tabs),
    )
    out, gin, wg = pl.pallas_call(
        writer,
        out_shape=shapes,
        in_specs=[any_spec] * 3,
        out_specs=[hbm] * 3,
        scratch_shapes=[pltpu.SemaphoreType.DMA((9,))],
        compiler_params=pltpu.CompilerParams(vmem_limit_bytes=1024 * 1024),
        name="write_results",
    )(*results)
    return (
        out.reshape(inputs.shape),
        gin.reshape(inputs.shape),
        wg.reshape(1, 2, 4, C, MY * MZ),
    )


def solution(mesh):
    field_spec = P("dp", "gx", None, None, None)
    in_specs = (field_spec, P("gx", None, None, None, None), P(), field_spec) + (P(),) * 5
    out_specs = (field_spec, field_spec, P("gx", None, "dp", None, None))
    mapped = jax.shard_map(
        per_device, mesh=mesh, in_specs=in_specs, out_specs=out_specs, check_vma=False
    )
    tabs = tables()

    def run(inputs, spectral_weights, skip_weights, cotangent):
        return mapped(
            inputs, spectral_weights, skip_weights, cotangent, *[jnp.asarray(t) for t in tabs]
        )

    return run
```

```python
import functools
import math

import jax
import jax.numpy as jnp
import ml_dtypes
import numpy as np
from jax import lax
from jax.experimental import pallas as pl
from jax.experimental.pallas import tpu as pltpu
from jax.sharding import PartitionSpec as P

MESH = pl.DeviceIdType.MESH
F32 = jnp.float32
BF16 = jnp.bfloat16

NX, NY, NZ, MX, MY, MZ, C = 128, 64, 128, 32, 16, 16, 32
GX, DP = 32, 8
SLAB = NX // GX
GRID_SCALE = 1.0 / math.sqrt(NX * NY * NZ)
MODE_SCALE = 1.0 / math.sqrt(MX * MY * MZ)
PIECE = (GX, 16, 128)
ROUNDS = (3, 2, 1, 0)


def angles(length, freqs):
    phase = (np.arange(length)[:, None] * freqs[None, :]) % length
    angle = np.float32(2.0 * math.pi / length) * phase.astype(np.float32)
    return np.cos(angle).astype(np.float32), np.sin(angle).astype(np.float32)


def signed(count):
    k = np.arange(count)
    return np.where(k < count // 2, k, k - count)


def tables():
    bf = ml_dtypes.bfloat16
    cz, sz = angles(NZ, np.arange(MZ))
    zt = np.zeros((MZ, 2, 8, 8, NZ), np.float32)
    for q in range(8):
        zt[:, 0, q, q, :] = cz.T
        zt[:, 1, q, q, :] = -sz.T
    cy, sy = angles(NY, signed(MY))
    yb = np.stack([cy, -sy], axis=1)
    lt = np.einsum("ybk,cd->ycbkd", yb, np.eye(16, dtype=np.float32))
    cx, sx = angles(NX, signed(MX))
    rot = np.stack([np.stack([cx, sx]), np.stack([-sx, cx])])
    rot = rot.reshape(2, 2, GX, SLAB, MX)
    xf = np.einsum("pagrk,hj->phkgajr", rot, np.eye(2, dtype=np.float32))
    xf = xf.reshape(128, 512)
    return (
        zt.reshape(256, 1024).astype(bf),
        np.ascontiguousarray(zt.reshape(256, 1024).T).astype(bf),
        lt.reshape(1024, 512).astype(bf),
        xf.astype(bf),
        np.ascontiguousarray(xf.T).astype(bf),
    )


def dot(a, b):
    return jnp.dot(a, b, preferred_element_type=F32)


def dot_nt(a, b):
    return lax.dot_general(a, b, (((1,), (1,)), ((), ())), preferred_element_type=F32)


def iota(shape, axis):
    return lax.broadcasted_iota(jnp.int32, shape, axis)


def swap16(x):
    _, rows, _ = x.shape
    for s in (1, 2, 4, 8):
        keep_low = (iota((rows, 128), 1) & s) == 0
        parts = [None] * 16
        for i in range(16):
            if i & s:
                continue
            low, high = x[i], x[i + s]
            parts[i] = jnp.where(keep_low, low, pltpu.roll(high, s, 1))
            parts[i + s] = jnp.where(keep_low, pltpu.roll(low, 128 - s, 1), high)
        x = parts if s == 8 else _Stack(parts, rows)
    return x


class _Stack:
    def __init__(self, parts, rows):
        self.parts, self.shape = parts, (16, rows, 128)

    def __getitem__(self, i):
        return self.parts[i]


def gelu_pair(x):
    k0 = math.sqrt(2.0 / math.pi)
    u = x * (k0 + (k0 * 0.044715) * (x * x))
    t = jnp.tanh(u)
    half = 0.5 * t + 0.5
    slope = half + (1.5 * u - k0 * x) * (1.0 - t * t)
    return x * half, slope


def kernel(
    x_hbm, w_hbm, s_hbm, ct_hbm, zt_hbm, zf_hbm, lt_hbm, xf_hbm, xi_hbm,
    out_hbm, gin_hbm, wg_hbm,
    f_v, ct_v, o_v, gp_v, zt_v, zf_v, lt_v, xf_v, xi_v, wl_v,
    sw, sa1, sd1, sa2, sd2, swg,
    ra1, rd1, ra2, rd2, rwg,
    wall, mall, ball,
    m_v, p_v, q_v, gx_v, e_v, sk_v, t_v, sk_w, wt_v, wo_v, ks_v, kb_v,
    lsem, ss, rs,
):
    me = lax.axis_index("gx")
    d = lax.axis_index("dp")
    bar = pltpu.get_barrier_semaphore()

    def peer(q):
        i, j = q // 4, lax.rem(q, 4)
        dz = 4 + (1 - 2 * lax.rem(i, 2)) * ((i + 1) // 2)
        dy = 2 + (1 - 2 * lax.rem(j, 2)) * ((j + 1) // 2)
        return lax.rem(me // 4 + dz, 8) * 4 + lax.rem(lax.rem(me, 4) + dy, 4)

    def greet_g(q, c):
        pl.semaphore_signal(bar, inc=1, device_id={"gx": peer(q)}, device_id_type=MESH)
        return c

    def greet_d(p, c):
        pl.semaphore_signal(bar, inc=1, device_id={"dp": lax.rem(d + p, DP)}, device_id_type=MESH)
        return c

    lax.fori_loop(0, GX - 1, greet_g, 0, unroll=True)
    lax.fori_loop(1, DP, greet_d, 0, unroll=True)

    pending = {}

    def load(name, src, dst, n):
        copy = pltpu.make_async_copy(src, dst, lsem.at[n])
        copy.start()
        pending[name] = copy.wait

    def settle(*names):
        for name in names:
            pending.pop(name)()

    def wait_bytes(ref, sem, count):
        view = ref.at[pl.ds(0, count)]
        pltpu.make_async_copy(view, view, sem).wait()

    def expect(name, n, ref, count):
        pending[name] = lambda: wait_bytes(ref, rs.at[n], count)
        pending[name + "_sent"] = lambda: wait_bytes(ref, ss.at[n], count)

    ih0, oh0 = lax.rem(d // 2, 2), lax.rem(d, 2)
    slot = 2 * ih0 + oh0
    other = lax.rem(slot + 2, 4)
    w_mine = w_hbm.at[:, pl.ds(ih0 * 16, 16), pl.ds(oh0 * 16, 16), :]
    load("w", w_mine, wl_v, 0)
    load("zf", zf_hbm, zf_v, 1)
    load("f", x_hbm, f_v, 2)
    load("lt", lt_hbm, lt_v, 3)
    load("s", s_hbm, sk_w, 11)
    load("xf", xf_hbm, xf_v, 4)
    load("xi", xi_hbm, xi_v, 5)
    load("zt", zt_hbm, zt_v, 10)
    load("ct", ct_hbm, ct_v, 6)

    def spread(name, send, recv, n):
        def body(q, c):
            t = peer(q)
            pltpu.make_async_remote_copy(
                send.at[t], recv.at[me], ss.at[n], rs.at[n],
                device_id={"gx": t}, device_id_type=MESH,
            ).start()
            return c

        lax.fori_loop(0, GX - 1, body, 0, unroll=True)
        recv[me] = send[me]
        expect(name, n, recv, GX - 1)

    def share(name, buf, n):
        def body(p, c):
            pltpu.make_async_remote_copy(
                buf.at[d], buf.at[d], ss.at[n], rs.at[n],
                device_id={"dp": lax.rem(d + p, DP)}, device_id_type=MESH,
            ).start()
            return c

        for p in (4, 5, 3, 6, 2, 7, 1):
            body(p, 0)
        expect(name, n, buf, DP - 1)

    settle("w")
    for a in range(2):
        for kyh in range(2):
            swapped = swap16(wl_v[a, :, :, kyh * 128:(kyh + 1) * 128].astype(F32))
            for kz in range(16):
                sw[kyh * 16 + kz, a] = swapped[kz].astype(BF16)

    def planes(field, send):
        for t in range(4):
            blocks = [
                field[x, pl.ds(t * 16, 16), h].reshape(256, 128)
                for h in range(2) for x in range(SLAB)
            ]
            along_z = dot(jnp.concatenate(blocks, axis=1), zf_v[...])
            t_v[:, t * 256:(t + 1) * 256] = along_z.T.astype(BF16)
        u = dot(t_v[...], lt_v[...])
        u = u.reshape(16, 2, 8, 512)
        u0, u1 = u[:, 0], u[:, 1]
        re = u0[:, :, :256] - u1[:, :, 256:]
        im = u0[:, :, 256:] + u1[:, :, :256]
        both = jnp.stack([re, im], axis=1).reshape(16, 16, 256).astype(BF16)
        send[0:16] = both[:, :, :128]
        send[16:32] = both[:, :, 128:]

    settle("zf", "lt", "f")
    planes(f_v, sa1)

    er = iota((256, 32), 0)
    expand = (lax.rem(er, 32) == iota((256, 32), 1)).astype(F32).astype(BF16)
    same = iota((256, 256), 0) // 32 == iota((256, 256), 1) // 32
    settle("s")
    sk = sk_w[...]
    es = dot(expand, sk).astype(BF16)
    kb_v[...] = jnp.where(same, dot_nt(es, expand), 0.0).astype(BF16)
    est = dot_nt(expand, sk).astype(BF16)
    ks_v[...] = jnp.where(same, dot_nt(est, expand), 0.0).astype(BF16)
    sum_l = (iota((64, 1024), 0) == iota((64, 1024), 1) // 16).astype(F32).astype(BF16)
    rep_l = (iota((1024, 64), 0) // 16 == iota((1024, 64), 1)).astype(F32).astype(BF16)
    ones_b = (iota((128, 128), 0) // 16 == iota((128, 128), 1) // 16).astype(F32).astype(BF16)
    diag = lax.rem(iota((1024, 128), 0), 16) == lax.rem(iota((1024, 128), 1), 16)


    pl.semaphore_wait(bar, GX - 1 + DP - 1)

    def body_w(q, c):
        t = peer(q)
        pltpu.make_async_remote_copy(
            sw.at[t], wall.at[slot, me], ss.at[0], rs.at[20 + q // 8],
            device_id={"gx": t}, device_id_type=MESH,
        ).start()
        return c

    for r in ROUNDS:
        lax.fori_loop(8 * r, min(8 * r + 8, GX - 1), body_w, 0, unroll=True)
    wall[slot, me] = sw[me]
    pending["weights_sent"] = lambda: wait_bytes(sw, ss.at[0], GX - 1)
    for r in ROUNDS:
        pending[f"weights_gx{r}"] = lambda r=r: wait_bytes(sw, rs.at[20 + r], min(8, GX - 1 - 8 * r))
    spread("a1", sa1, ra1, 1)

    mate = d + 1 - 2 * lax.rem(d, 2)

    def gather(s, i, target, send_n, recv_n):
        dz = 4 + (1 - 2 * (i % 2)) * ((i + 1) // 2)
        z = lax.rem(me // 4 + 8 - dz, 8)
        block = wall.at[s, pl.ds(4 * z, 4)]
        pltpu.make_async_remote_copy(
            block, block, ss.at[send_n], rs.at[recv_n],
            device_id={"dp": target}, device_id_type=MESH,
        ).start()

    for r in ROUNDS:
        settle(f"weights_gx{r}")
        gather(slot, 2 * r, lax.rem(d + 2, DP), 2, 24 + 2 * r)
        gather(slot, 2 * r + 1, lax.rem(d + 6, DP), 2, 25 + 2 * r)
        for i in (2 * r, 2 * r + 1):
            gather(slot, i, mate, 3, 3)

    def four(sem):
        view = wall.at[0, pl.ds(0, 4)]
        pltpu.make_async_copy(view, view, sem).wait()

    for i in range(8):
        pending[f"weights_x{i}"] = lambda i=i: four(rs.at[24 + i])
    pending["weights_x_sent"] = lambda: wait_bytes(wall, ss.at[2], 1)

    def pass_on(rounds):
        for r in rounds:
            for i in (2 * r, 2 * r + 1):
                settle(f"weights_x{i}")
                gather(other, i, mate, 3, 3)

    pass_on(ROUNDS[:2])

    def to_modes(recv, scale):
        r = recv[...].reshape(512, 128)
        return (dot(xf_v[...], r) * scale).astype(BF16)

    def to_slabs(mixed, send):
        send[...] = dot(xi_v[...], mixed).astype(BF16).reshape(PIECE)

    settle("xf", "xi", "a1")
    modes = to_modes(ra1, GRID_SCALE)
    mall[d] = modes
    m_v[...] = modes.astype(F32)

    pass_on(ROUNDS[2:])
    expect("weights_core", 3, wall, 2)
    settle("weights_core")

    def weight(a, h, oh, k):
        return wall[2 * h + oh, k, a].astype(F32)

    def mix(k, c):
        mr = [m_v[pl.ds(h * 32 + k, 1), :] for h in range(2)]
        mi = [m_v[pl.ds(64 + h * 32 + k, 1), :] for h in range(2)]
        for oh in range(2):
            re = im = None
            for h in range(2):
                wr, wi = weight(0, h, oh, k), weight(1, h, oh, k)
                r = wr * mr[h] - wi * mi[h]
                i = wr * mi[h] + wi * mr[h]
                re = r if re is None else re + r
                im = i if im is None else im + i
            row = pl.multiple_of(oh * 512 + k * 16, 16)
            p_v[0, pl.ds(row, 16), :] = re.astype(BF16)
            p_v[1, pl.ds(row, 16), :] = im.astype(BF16)
        return c

    lax.fori_loop(0, MX, mix, 0, unroll=8)
    mixed = []
    for a in range(2):
        q = jnp.where(diag, dot(p_v[a], ones_b), 0.0).astype(BF16)
        mixed.append(dot(sum_l, q))
    to_slabs(jnp.concatenate(mixed, axis=0).astype(BF16), sd1)
    spread("d1", sd1, rd1, 5)

    def unpack(recv):
        g = recv[...].astype(F32)
        g = jnp.concatenate([g[:16], g[16:]], axis=2).reshape(16, 2, 8, 256)
        turned = jnp.stack([g[:, 1], -g[:, 0]], axis=1).reshape(256, 256)
        gx_v[0:256, :] = g.reshape(256, 256).T.astype(BF16)
        gx_v[256:512, :] = turned.T.astype(BF16)

    def skips(source, channel_map):
        def body(t, c):
            for x in range(0, SLAB, 2):
                src = jnp.concatenate(
                    [source[x + i, pl.ds(t * 8, 8)].reshape(256, 128) for i in range(2)], axis=1
                )
                skip = dot(channel_map[...], src).reshape(8, 2, 16, 256)
                for i in range(2):
                    sk_v[x + i, pl.ds(t * 8, 8)] = skip[..., i * 128:(i + 1) * 128]
            return c

        lax.fori_loop(0, 8, body, 0)

    def fields(scale, emit):
        for t in range(4):
            vt = (dot(lt_v[t * 256:(t + 1) * 256, :], gx_v[...]) * scale).astype(BF16)
            for x in range(0, SLAB, 2):
                for h in range(2):
                    lo = (h * 4 + x) * 128
                    fld = dot(vt, zt_v[:, lo:lo + 256]).reshape(16, 16, 256)
                    for i in range(2):
                        rows = pl.ds(t * 16, 16)
                        total = fld[:, :, i * 128:(i + 1) * 128] + sk_v[x + i, rows, h]
                        emit(x + i, rows, h, total)

    share("mall", mall, 4)
    skips(f_v, ks_v)
    settle("ct", "zt", "d1")
    unpack(rd1)

    def emit_forward(x, rows, h, pre):
        act, slope = gelu_pair(pre)
        o_v[x, rows, h] = act.astype(BF16)
        gp_v[x, rows, h] = (ct_v[x, rows, h].astype(F32) * slope).astype(BF16)

    fields(MODE_SCALE, emit_forward)
    load("out", o_v, out_hbm, 7)

    planes(gp_v, sa2)
    spread("a2", sa2, ra2, 6)
    skips(gp_v, kb_v)
    settle("a2")
    back = to_modes(ra2, MODE_SCALE)
    ball[d] = back
    share("ball", ball, 7)

    for a in range(2):
        rows = jnp.where(diag, dot(rep_l, back[64 * a:64 * a + 64]), 0.0).astype(BF16)
        q_v[a] = dot(rows, ones_b)

    def conj_mix(k, c):
        for h in range(2):
            re = im = None
            for oh in range(2):
                row = pl.multiple_of(oh * 512 + k * 16, 16)
                br, bi = q_v[0, pl.ds(row, 16), :], q_v[1, pl.ds(row, 16), :]
                wr, wi = weight(0, h, oh, k), weight(1, h, oh, k)
                r = wr * br + wi * bi
                i = wr * bi - wi * br
                re = r if re is None else re + r
                im = i if im is None else im + i
            row = pl.multiple_of(h * 512 + k * 16, 16)
            p_v[0, pl.ds(row, 16), :] = re.astype(BF16)
            p_v[1, pl.ds(row, 16), :] = im.astype(BF16)
        return c

    lax.fori_loop(0, MX, conj_mix, 0, unroll=8)
    back_modes = [dot(sum_l, p_v[a]) for a in range(2)]
    to_slabs(jnp.concatenate(back_modes, axis=0).astype(BF16), sd2)
    spread("d2", sd2, rd2, 8)

    settle("mall")
    sel_r, sel_c = iota((128, 512), 0), iota((128, 512), 1)
    chan = 4 * lax.rem(d, 4) + sel_c // 128
    pick = (lax.rem(sel_r, 16) == chan) & (sel_r // 16 == lax.rem(sel_c, 128) // 16)
    pick = pick.astype(F32).astype(BF16)
    ihd = d // 4
    for a in range(2):
        start = pl.multiple_of(a * 64 + ihd * 32, 32)
        rows = mall[:, pl.ds(start, 32), :].reshape(256, 128)
        e_v[a] = dot(rows, pick)
    settle("ball")
    for oh in range(2):
        for i4 in range(4):
            def add(n, acc):
                re, im = acc
                row = pl.multiple_of(n * 32, 32)
                er_ = e_v[0, pl.ds(row, 32), i4 * 128:(i4 + 1) * 128]
                ei_ = e_v[1, pl.ds(row, 32), i4 * 128:(i4 + 1) * 128]
                br = ball[n, oh * 32:oh * 32 + 32, :].astype(F32)
                bi = ball[n, 64 + oh * 32:64 + oh * 32 + 32, :].astype(F32)
                return re + er_ * br + ei_ * bi, im + er_ * bi - ei_ * br

            zero = jnp.zeros((32, 128), F32)
            re, im = lax.fori_loop(0, DP, add, (zero, zero), unroll=True)
            wt_v[:, i4 * 2 + oh, :] = re
            wt_v[:, 8 + i4 * 2 + oh, :] = im
    swg[...] = wt_v[...].astype(BF16)
    spread("wg", swg, rwg, 9)

    settle("d2", "out")
    unpack(rd2)

    def emit_backward(x, rows, h, total):
        o_v[x, rows, h] = total.astype(BF16)

    fields(GRID_SCALE, emit_backward)
    load("gin", o_v, gin_hbm, 8)

    settle("wg")
    for kyh in range(2):
        swapped = swap16(rwg[kyh * 16:kyh * 16 + 16].astype(F32))
        for o in range(16):
            wo_v[:, o, kyh * 128:(kyh + 1) * 128] = swapped[o]
    load("wg_out", wo_v, wg_hbm, 9)
    settle(*list(pending))


def writer(out_a, gin_a, wg_a, out_b, gin_b, wg_b, sem):
    pairs = [(a.at[i], b.at[i]) for a, b in ((out_a, out_b), (gin_a, gin_b)) for i in range(SLAB)]
    pairs.append((wg_a, wg_b))
    copies = [pltpu.make_async_copy(a, b, sem.at[n]) for n, (a, b) in enumerate(pairs)]
    for copy in copies:
        copy.start()
    for copy in copies:
        copy.wait()


def per_device(inputs, spectral_weights, skip_weights, cotangent, *tabs):
    shape5 = (SLAB, NY, 2, 16, NZ)
    any_spec = pl.BlockSpec(memory_space=pl.ANY)
    vm = pltpu.VMEM
    big = vm(shape5, BF16)
    piece = vm(PIECE, BF16)
    hbm = pl.BlockSpec(memory_space=pltpu.HBM)
    keep = functools.partial(pltpu.with_memory_space_constraint, memory_space=pltpu.HBM)
    shapes = [
        jax.ShapeDtypeStruct(shape5, BF16),
        jax.ShapeDtypeStruct(shape5, BF16),
        jax.ShapeDtypeStruct((16, 16, 256), F32),
    ]
    results = pl.pallas_call(
        kernel,
        out_shape=[vm(s.shape, s.dtype) for s in shapes],
        in_specs=[hbm] * 9,
        out_specs=[any_spec] * 3,
        scratch_shapes=[
            big, big, big, big,
            vm((256, 1024), BF16), vm((1024, 256), BF16), vm((1024, 512), BF16),
            vm((128, 512), BF16), vm((512, 128), BF16),
            vm((2, 16, 16, 256), BF16),
            vm((GX, 2, 16, 128), BF16), *([piece] * 10),
            vm((4, GX, 2, 16, 128), BF16), vm((DP, 128, 128), BF16), vm((DP, 128, 128), BF16),
            vm((128, 128), F32), vm((2, 1024, 128), BF16), vm((2, 1024, 128), F32),
            vm((512, 256), BF16), vm((2, 256, 512), F32), vm(shape5, F32), vm((256, 1024), BF16), vm((32, 32), BF16),
            vm(PIECE, F32), vm((16, 16, 256), F32),
            vm((256, 256), BF16), vm((256, 256), BF16),
            pltpu.SemaphoreType.DMA((36,)),
            pltpu.SemaphoreType.DMA((36,)),
            pltpu.SemaphoreType.DMA((36,)),
        ],
        compiler_params=pltpu.CompilerParams(
            collective_id=0, has_side_effects=True, vmem_limit_bytes=40 * 1024 * 1024
        ),
        cost_estimate=pl.CostEstimate(flops=8_000_000_000, bytes_accessed=12_000_000, transcendentals=1_048_576),
        name="spectral_layer",
    )(
        keep(inputs.reshape(shape5)), keep(spectral_weights[0]), keep(skip_weights),
        keep(cotangent.reshape(shape5)), *map(keep, tabs),
    )
    out, gin, wg = pl.pallas_call(
        writer,
        out_shape=shapes,
        in_specs=[any_spec] * 3,
        out_specs=[hbm] * 3,
        scratch_shapes=[pltpu.SemaphoreType.DMA((9,))],
        compiler_params=pltpu.CompilerParams(vmem_limit_bytes=1024 * 1024),
        name="write_results",
    )(*results)
    return (
        out.reshape(inputs.shape),
        gin.reshape(inputs.shape),
        wg.reshape(1, 2, 4, C, MY * MZ),
    )


def solution(mesh):
    field_spec = P("dp", "gx", None, None, None)
    in_specs = (field_spec, P("gx", None, None, None, None), P(), field_spec) + (P(),) * 5
    out_specs = (field_spec, field_spec, P("gx", None, "dp", None, None))
    mapped = jax.shard_map(
        per_device, mesh=mesh, in_specs=in_specs, out_specs=out_specs, check_vma=False
    )
    tabs = tables()

    def run(inputs, spectral_weights, skip_weights, cotangent):
        return mapped(
            inputs, spectral_weights, skip_weights, cotangent, *[jnp.asarray(t) for t in tabs]
        )

    return run
```

```python
import functools
import math

import jax
import jax.numpy as jnp
import ml_dtypes
import numpy as np
from jax import lax
from jax.experimental import pallas as pl
from jax.experimental.pallas import tpu as pltpu
from jax.sharding import PartitionSpec as P

MESH = pl.DeviceIdType.MESH
F32 = jnp.float32
BF16 = jnp.bfloat16

NX, NY, NZ, MX, MY, MZ, C = 128, 64, 128, 32, 16, 16, 32
GX, DP = 32, 8
SLAB = NX // GX
GRID_SCALE = 1.0 / math.sqrt(NX * NY * NZ)
MODE_SCALE = 1.0 / math.sqrt(MX * MY * MZ)
PIECE = (GX, 16, 128)
ROUNDS = (3, 2, 1, 0)


def angles(length, freqs):
    phase = (np.arange(length)[:, None] * freqs[None, :]) % length
    angle = np.float32(2.0 * math.pi / length) * phase.astype(np.float32)
    return np.cos(angle).astype(np.float32), np.sin(angle).astype(np.float32)


def signed(count):
    k = np.arange(count)
    return np.where(k < count // 2, k, k - count)


def tables():
    bf = ml_dtypes.bfloat16
    cz, sz = angles(NZ, np.arange(MZ))
    zt = np.zeros((MZ, 2, 8, 8, NZ), np.float32)
    for q in range(8):
        zt[:, 0, q, q, :] = cz.T
        zt[:, 1, q, q, :] = -sz.T
    cy, sy = angles(NY, signed(MY))
    yb = np.stack([cy, -sy], axis=1)
    lt = np.einsum("ybk,cd->ycbkd", yb, np.eye(16, dtype=np.float32))
    cx, sx = angles(NX, signed(MX))
    rot = np.stack([np.stack([cx, sx]), np.stack([-sx, cx])])
    rot = rot.reshape(2, 2, GX, SLAB, MX)
    xf = np.einsum("pagrk,hj->phkgajr", rot, np.eye(2, dtype=np.float32))
    xf = xf.reshape(128, 512)
    return (
        zt.reshape(256, 1024).astype(bf),
        np.ascontiguousarray(zt.reshape(256, 1024).T).astype(bf),
        lt.reshape(1024, 512).astype(bf),
        xf.astype(bf),
        np.ascontiguousarray(xf.T).astype(bf),
    )


def dot(a, b):
    return jnp.dot(a, b, preferred_element_type=F32)


def dot_nt(a, b):
    return lax.dot_general(a, b, (((1,), (1,)), ((), ())), preferred_element_type=F32)


def iota(shape, axis):
    return lax.broadcasted_iota(jnp.int32, shape, axis)


def swap16(x):
    _, rows, _ = x.shape
    for s in (1, 2, 4, 8):
        keep_low = (iota((rows, 128), 1) & s) == 0
        parts = [None] * 16
        for i in range(16):
            if i & s:
                continue
            low, high = x[i], x[i + s]
            parts[i] = jnp.where(keep_low, low, pltpu.roll(high, s, 1))
            parts[i + s] = jnp.where(keep_low, pltpu.roll(low, 128 - s, 1), high)
        x = parts if s == 8 else _Stack(parts, rows)
    return x


class _Stack:
    def __init__(self, parts, rows):
        self.parts, self.shape = parts, (16, rows, 128)

    def __getitem__(self, i):
        return self.parts[i]


def gelu_pair(x):
    k0 = math.sqrt(2.0 / math.pi)
    u = x * (k0 + (k0 * 0.044715) * (x * x))
    t = jnp.tanh(u)
    half = 0.5 * t + 0.5
    slope = half + (1.5 * u - k0 * x) * (1.0 - t * t)
    return x * half, slope


def kernel(
    x_hbm, w_hbm, s_hbm, ct_hbm, zt_hbm, zf_hbm, lt_hbm, xf_hbm, xi_hbm,
    out_hbm, gin_hbm, wg_hbm,
    f_v, ct_v, o_v, gp_v, zt_v, zf_v, lt_v, xf_v, xi_v, wl_v,
    sw, sa1, sd1, sa2, sd2, swg,
    ra1, rd1, ra2, rd2, rwg,
    wall, mall, ball,
    m_v, p_v, q_v, gx_v, e_v, sk_v, t_v, sk_w, wt_v, ks_v, kb_v,
    lsem, ss, rs,
):
    me = lax.axis_index("gx")
    d = lax.axis_index("dp")
    bar = pltpu.get_barrier_semaphore()

    def peer(q):
        i, j = q // 4, lax.rem(q, 4)
        dz = 4 + (1 - 2 * lax.rem(i, 2)) * ((i + 1) // 2)
        dy = 2 + (1 - 2 * lax.rem(j, 2)) * ((j + 1) // 2)
        return lax.rem(me // 4 + dz, 8) * 4 + lax.rem(lax.rem(me, 4) + dy, 4)

    def greet_g(q, c):
        pl.semaphore_signal(bar, inc=1, device_id={"gx": peer(q)}, device_id_type=MESH)
        return c

    def greet_d(p, c):
        pl.semaphore_signal(bar, inc=1, device_id={"dp": lax.rem(d + p, DP)}, device_id_type=MESH)
        return c

    pending = {}

    def load(name, src, dst, n):
        copy = pltpu.make_async_copy(src, dst, lsem.at[n])
        copy.start()
        pending[name] = copy.wait

    def settle(*names):
        for name in names:
            pending.pop(name)()

    def wait_bytes(ref, sem, count):
        view = ref.at[pl.ds(0, count)]
        pltpu.make_async_copy(view, view, sem).wait()

    def expect(name, n, ref, count):
        pending[name] = lambda: wait_bytes(ref, rs.at[n], count)
        pending[name + "_sent"] = lambda: wait_bytes(ref, ss.at[n], count)

    part, ih0, oh0 = d // 4, lax.rem(d // 2, 2), lax.rem(d, 2)
    w_mine = w_hbm.at[part, pl.ds(ih0 * 16, 16), pl.ds(oh0 * 16, 16), :]
    load("w", w_mine, wl_v, 0)
    lax.fori_loop(0, GX - 1, greet_g, 0, unroll=True)
    lax.fori_loop(1, DP, greet_d, 0, unroll=True)
    load("zf", zf_hbm, zf_v, 1)
    load("f", x_hbm, f_v, 2)
    load("lt", lt_hbm, lt_v, 3)
    load("s", s_hbm, sk_w, 11)
    load("xf", xf_hbm, xf_v, 4)
    load("xi", xi_hbm, xi_v, 5)
    load("zt", zt_hbm, zt_v, 10)
    load("ct", ct_hbm, ct_v, 6)

    def spread(name, send, recv, n):
        def body(q, c):
            t = peer(q)
            pltpu.make_async_remote_copy(
                send.at[t], recv.at[me], ss.at[n], rs.at[n],
                device_id={"gx": t}, device_id_type=MESH,
            ).start()
            return c

        lax.fori_loop(0, GX - 1, body, 0, unroll=True)
        recv[me] = send[me]
        expect(name, n, recv, GX - 1)

    def share(name, buf, n):
        def body(p, c):
            pltpu.make_async_remote_copy(
                buf.at[d], buf.at[d], ss.at[n], rs.at[n],
                device_id={"dp": lax.rem(d + p, DP)}, device_id_type=MESH,
            ).start()
            return c

        for p in (4, 5, 3, 6, 2, 7, 1):
            body(p, 0)
        expect(name, n, buf, DP - 1)

    settle("w")
    for kyh in range(2):
        swapped = swap16(wl_v[:, :, kyh * 128:(kyh + 1) * 128].astype(F32))
        for kz in range(16):
            sw[kyh * 16 + kz] = swapped[kz].astype(BF16)

    def planes(field, send):
        for t in range(4):
            blocks = [
                field[x, pl.ds(t * 16, 16), h].reshape(256, 128)
                for h in range(2) for x in range(SLAB)
            ]
            along_z = dot(jnp.concatenate(blocks, axis=1), zf_v[...])
            t_v[:, t * 256:(t + 1) * 256] = along_z.T.astype(BF16)
        u = dot(t_v[...], lt_v[...])
        u = u.reshape(16, 2, 8, 512)
        u0, u1 = u[:, 0], u[:, 1]
        re = u0[:, :, :256] - u1[:, :, 256:]
        im = u0[:, :, 256:] + u1[:, :, :256]
        both = jnp.stack([re, im], axis=1).reshape(16, 16, 256).astype(BF16)
        send[0:16] = both[:, :, :128]
        send[16:32] = both[:, :, 128:]

    pl.semaphore_wait(bar, GX - 1 + DP - 1)

    def body_w(q, c):
        t = peer(q)
        pltpu.make_async_remote_copy(
            sw.at[t], wall.at[d, me], ss.at[0], rs.at[20 + q // 8],
            device_id={"gx": t}, device_id_type=MESH,
        ).start()
        return c

    for r in ROUNDS:
        lax.fori_loop(8 * r, min(8 * r + 8, GX - 1), body_w, 0, unroll=True)
    wall[d, me] = sw[me]
    pending["weights_sent"] = lambda: wait_bytes(sw, ss.at[0], GX - 1)
    for r in ROUNDS:
        pending[f"weights_gx{r}"] = lambda r=r: wait_bytes(sw, rs.at[20 + r], min(8, GX - 1 - 8 * r))
    settle("zf", "lt", "f")
    planes(f_v, sa1)
    spread("a1", sa1, ra1, 1)

    er = iota((256, 32), 0)
    expand = (lax.rem(er, 32) == iota((256, 32), 1)).astype(F32).astype(BF16)
    same = iota((256, 256), 0) // 32 == iota((256, 256), 1) // 32
    settle("s")
    sk = sk_w[...]
    es = dot(expand, sk).astype(BF16)
    kb_v[...] = jnp.where(same, dot_nt(es, expand), 0.0).astype(BF16)
    est = dot_nt(expand, sk).astype(BF16)
    ks_v[...] = jnp.where(same, dot_nt(est, expand), 0.0).astype(BF16)
    sum_l = (iota((64, 1024), 0) == iota((64, 1024), 1) // 16).astype(F32).astype(BF16)
    rep_l = (iota((1024, 64), 0) // 16 == iota((1024, 64), 1)).astype(F32).astype(BF16)
    ones_b = (iota((128, 128), 0) // 16 == iota((128, 128), 1) // 16).astype(F32).astype(BF16)
    diag = lax.rem(iota((1024, 128), 0), 16) == lax.rem(iota((1024, 128), 1), 16)


    mate = d + 1 - 2 * lax.rem(d, 2)

    def block_z(i):
        return lax.rem(me // 4 + 4 - (1 - 2 * (i % 2)) * ((i + 1) // 2), 8)

    def gather(s, i, target, send_n, recv_n):
        z = block_z(i)
        block = wall.at[s, pl.ds(4 * z, 4)]
        pltpu.make_async_remote_copy(
            block, block, ss.at[send_n], rs.at[recv_n],
            device_id={"dp": target}, device_id_type=MESH,
        ).start()

    for r in ROUNDS:
        settle(f"weights_gx{r}")
        for p in (2, 1, 3):
            for i in (2 * r, 2 * r + 1):
                gather(d, i, lax.rem(d + 2 * p, DP), 2, 24 + 3 * r + p - 1)
        for i in (2 * r, 2 * r + 1):
            gather(d, i, mate, 3, 36 + r)

    for r in ROUNDS:
        for p in (1, 3, 2):
            pending[f"weights_x{r}{p}"] = lambda n=24 + 3 * r + p - 1: wait_bytes(wall.at[0], rs.at[n], 8)
        pending[f"weights_core{r}"] = lambda r=r: wait_bytes(wall.at[0], rs.at[36 + r], GX)
    pending["weights_x_sent"] = lambda: wait_bytes(wall, ss.at[2], 3)
    pending["weights_core_sent"] = lambda: wait_bytes(wall, ss.at[3], 4)
    for r in ROUNDS:
        for p in (1, 3, 2):
            settle(f"weights_x{r}{p}")
            for i in (2 * r, 2 * r + 1):
                gather(lax.rem(d + 8 - 2 * p, DP), i, mate, 3, 36 + r)

    def to_modes(recv, scale):
        r = recv[...].reshape(512, 128)
        return (dot(xf_v[...], r) * scale).astype(BF16)

    def to_slabs(mixed, send):
        send[...] = dot(xi_v[...], mixed).astype(BF16).reshape(PIECE)

    settle("xf", "xi", "a1")
    modes = to_modes(ra1, GRID_SCALE)
    mall[d] = modes
    m_v[...] = modes.astype(F32)


    def weight(a, h, oh, k):
        return wall[4 * a + 2 * h + oh, k].astype(F32)

    def mix(k, c):
        mr = [m_v[pl.ds(h * 32 + k, 1), :] for h in range(2)]
        mi = [m_v[pl.ds(64 + h * 32 + k, 1), :] for h in range(2)]
        for oh in range(2):
            re = im = None
            for h in range(2):
                wr, wi = weight(0, h, oh, k), weight(1, h, oh, k)
                r = wr * mr[h] - wi * mi[h]
                i = wr * mi[h] + wi * mr[h]
                re = r if re is None else re + r
                im = i if im is None else im + i
            row = pl.multiple_of(oh * 512 + k * 16, 16)
            p_v[0, pl.ds(row, 16), :] = re.astype(BF16)
            p_v[1, pl.ds(row, 16), :] = im.astype(BF16)
        return c

    for r in ROUNDS:
        settle(f"weights_core{r}")
        for i in (2 * r, 2 * r + 1):
            first = 4 * block_z(i)
            lax.fori_loop(0, 4, lambda j, c: mix(first + j, c), 0, unroll=True)
    mixed = []
    for a in range(2):
        q = jnp.where(diag, dot(p_v[a], ones_b), 0.0).astype(BF16)
        mixed.append(dot(sum_l, q))
    to_slabs(jnp.concatenate(mixed, axis=0).astype(BF16), sd1)
    spread("d1", sd1, rd1, 5)

    def unpack(recv):
        g = recv[...].astype(F32)
        g = jnp.concatenate([g[:16], g[16:]], axis=2).reshape(16, 2, 8, 256)
        turned = jnp.stack([g[:, 1], -g[:, 0]], axis=1).reshape(256, 256)
        gx_v[0:256, :] = g.reshape(256, 256).T.astype(BF16)
        gx_v[256:512, :] = turned.T.astype(BF16)

    def skips(source, channel_map):
        def body(t, c):
            for x in range(0, SLAB, 2):
                src = jnp.concatenate(
                    [source[x + i, pl.ds(t * 8, 8)].reshape(256, 128) for i in range(2)], axis=1
                )
                skip = dot(channel_map[...], src).reshape(8, 2, 16, 256)
                for i in range(2):
                    sk_v[x + i, pl.ds(t * 8, 8)] = skip[..., i * 128:(i + 1) * 128]
            return c

        lax.fori_loop(0, 8, body, 0)

    def fields(scale, emit):
        for t in range(4):
            vt = (dot(lt_v[t * 256:(t + 1) * 256, :], gx_v[...]) * scale).astype(BF16)
            for x in range(0, SLAB, 2):
                for h in range(2):
                    lo = (h * 4 + x) * 128
                    fld = dot(vt, zt_v[:, lo:lo + 256]).reshape(16, 16, 256)
                    for i in range(2):
                        rows = pl.ds(t * 16, 16)
                        total = fld[:, :, i * 128:(i + 1) * 128] + sk_v[x + i, rows, h]
                        emit(x + i, rows, h, total)

    share("mall", mall, 4)
    skips(f_v, ks_v)
    settle("ct", "zt", "d1")
    unpack(rd1)

    def emit_forward(x, rows, h, pre):
        act, slope = gelu_pair(pre)
        o_v[x, rows, h] = act.astype(BF16)
        gp_v[x, rows, h] = (ct_v[x, rows, h].astype(F32) * slope).astype(BF16)

    fields(MODE_SCALE, emit_forward)
    load("out", o_v, out_hbm, 7)

    planes(gp_v, sa2)
    spread("a2", sa2, ra2, 6)
    skips(gp_v, kb_v)
    settle("a2")
    back = to_modes(ra2, MODE_SCALE)
    ball[d] = back
    share("ball", ball, 7)

    for a in range(2):
        rows = jnp.where(diag, dot(rep_l, back[64 * a:64 * a + 64]), 0.0).astype(BF16)
        q_v[a] = dot(rows, ones_b)

    def conj_mix(k, c):
        for h in range(2):
            re = im = None
            for oh in range(2):
                row = pl.multiple_of(oh * 512 + k * 16, 16)
                br, bi = q_v[0, pl.ds(row, 16), :], q_v[1, pl.ds(row, 16), :]
                wr, wi = weight(0, h, oh, k), weight(1, h, oh, k)
                r = wr * br + wi * bi
                i = wr * bi - wi * br
                re = r if re is None else re + r
                im = i if im is None else im + i
            row = pl.multiple_of(h * 512 + k * 16, 16)
            p_v[0, pl.ds(row, 16), :] = re.astype(BF16)
            p_v[1, pl.ds(row, 16), :] = im.astype(BF16)
        return c

    lax.fori_loop(0, MX, conj_mix, 0, unroll=8)
    back_modes = [dot(sum_l, p_v[a]) for a in range(2)]
    to_slabs(jnp.concatenate(back_modes, axis=0).astype(BF16), sd2)
    spread("d2", sd2, rd2, 8)

    settle("mall")
    sel_r, sel_c = iota((128, 512), 0), iota((128, 512), 1)
    chan = 4 * lax.rem(d, 4) + sel_c // 128
    pick = (lax.rem(sel_r, 16) == chan) & (sel_r // 16 == lax.rem(sel_c, 128) // 16)
    pick = pick.astype(F32).astype(BF16)
    ihd = d // 4
    for a in range(2):
        start = pl.multiple_of(a * 64 + ihd * 32, 32)
        rows = mall[:, pl.ds(start, 32), :].reshape(256, 128)
        e_v[a] = dot(rows, pick)
    settle("ball")
    for oh in range(2):
        for i4 in range(4):
            def add(n, acc):
                re, im = acc
                row = pl.multiple_of(n * 32, 32)
                er_ = e_v[0, pl.ds(row, 32), i4 * 128:(i4 + 1) * 128]
                ei_ = e_v[1, pl.ds(row, 32), i4 * 128:(i4 + 1) * 128]
                br = ball[n, oh * 32:oh * 32 + 32, :].astype(F32)
                bi = ball[n, 64 + oh * 32:64 + oh * 32 + 32, :].astype(F32)
                return re + er_ * br + ei_ * bi, im + er_ * bi - ei_ * br

            zero = jnp.zeros((32, 128), F32)
            re, im = lax.fori_loop(0, DP, add, (zero, zero), unroll=True)
            wt_v[:, i4 * 2 + oh, :] = re
            wt_v[:, 8 + i4 * 2 + oh, :] = im
    swg[...] = wt_v[...].astype(BF16)
    spread("wg", swg, rwg, 9)

    settle("d2", "out")
    unpack(rd2)

    def emit_backward(x, rows, h, total):
        o_v[x, rows, h] = total.astype(BF16)

    fields(GRID_SCALE, emit_backward)
    load("gin", o_v, gin_hbm, 8)

    settle("wg")
    load("wg_out", rwg, wg_hbm, 9)
    settle(*list(pending))


def writer(out_a, gin_a, wg_a, out_b, gin_b, wg_b, pieces, wo_v, sem):
    first = pltpu.make_async_copy(wg_a, pieces, sem.at[9])
    first.start()
    pairs = [(a.at[i], b.at[i]) for a, b in ((out_a, out_b), (gin_a, gin_b)) for i in range(SLAB)]
    copies = [pltpu.make_async_copy(a, b, sem.at[n]) for n, (a, b) in enumerate(pairs)]
    for copy in copies:
        copy.start()
    first.wait()
    for kyh in range(2):
        swapped = swap16(pieces[kyh * 16:kyh * 16 + 16].astype(F32))
        for o in range(16):
            wo_v[:, o, kyh * 128:(kyh + 1) * 128] = swapped[o]
    last = pltpu.make_async_copy(wo_v, wg_b, sem.at[8])
    last.start()
    for copy in copies:
        copy.wait()
    last.wait()


def per_device(inputs, spectral_weights, skip_weights, cotangent, *tabs):
    shape5 = (SLAB, NY, 2, 16, NZ)
    any_spec = pl.BlockSpec(memory_space=pl.ANY)
    vm = pltpu.VMEM
    big = vm(shape5, BF16)
    piece = vm(PIECE, BF16)
    hbm = pl.BlockSpec(memory_space=pltpu.HBM)
    keep = functools.partial(pltpu.with_memory_space_constraint, memory_space=pltpu.HBM)
    shapes = [
        jax.ShapeDtypeStruct(shape5, BF16),
        jax.ShapeDtypeStruct(shape5, BF16),
        jax.ShapeDtypeStruct((16, 16, 256), F32),
    ]
    results = pl.pallas_call(
        kernel,
        out_shape=[vm(shape5, BF16), vm(shape5, BF16), piece],
        in_specs=[hbm] * 9,
        out_specs=[any_spec] * 3,
        scratch_shapes=[
            big, big, big, big,
            vm((256, 1024), BF16), vm((1024, 256), BF16), vm((1024, 512), BF16),
            vm((128, 512), BF16), vm((512, 128), BF16),
            vm((16, 16, 256), BF16),
            *([piece] * 11),
            vm((DP, *PIECE), BF16), vm((DP, 128, 128), BF16), vm((DP, 128, 128), BF16),
            vm((128, 128), F32), vm((2, 1024, 128), BF16), vm((2, 1024, 128), F32),
            vm((512, 256), BF16), vm((2, 256, 512), F32), vm(shape5, F32), vm((256, 1024), BF16), vm((32, 32), BF16),
            vm(PIECE, F32),
            vm((256, 256), BF16), vm((256, 256), BF16),
            *([pltpu.SemaphoreType.DMA((40,))] * 3),
        ],
        compiler_params=pltpu.CompilerParams(
            collective_id=0, has_side_effects=True, vmem_limit_bytes=40 * 1024 * 1024
        ),
        cost_estimate=pl.CostEstimate(flops=8_000_000_000, bytes_accessed=12_000_000, transcendentals=1_048_576),
        name="spectral_layer",
    )(
        keep(inputs.reshape(shape5)), keep(spectral_weights[0]), keep(skip_weights),
        keep(cotangent.reshape(shape5)), *map(keep, tabs),
    )
    out, gin, wg = pl.pallas_call(
        writer,
        out_shape=shapes,
        in_specs=[any_spec] * 3,
        out_specs=[hbm] * 3,
        scratch_shapes=[piece, vm((16, 16, 256), F32), pltpu.SemaphoreType.DMA((10,))],
        compiler_params=pltpu.CompilerParams(vmem_limit_bytes=4 * 1024 * 1024),
        name="write_results",
    )(*results)
    return (
        out.reshape(inputs.shape),
        gin.reshape(inputs.shape),
        wg.reshape(1, 2, 4, C, MY * MZ),
    )


def solution(mesh):
    field_spec = P("dp", "gx", None, None, None)
    in_specs = (field_spec, P("gx", None, None, None, None), P(), field_spec) + (P(),) * 5
    out_specs = (field_spec, field_spec, P("gx", None, "dp", None, None))
    mapped = jax.shard_map(
        per_device, mesh=mesh, in_specs=in_specs, out_specs=out_specs, check_vma=False
    )
    tabs = tables()

    def run(inputs, spectral_weights, skip_weights, cotangent):
        return mapped(
            inputs, spectral_weights, skip_weights, cotangent, *[jnp.asarray(t) for t in tabs]
        )

    return run
```

```python
import functools
import math

import jax
import jax.numpy as jnp
import ml_dtypes
import numpy as np
from jax import lax
from jax.experimental import pallas as pl
from jax.experimental.pallas import tpu as pltpu
from jax.sharding import PartitionSpec as P

MESH = pl.DeviceIdType.MESH
F32 = jnp.float32
BF16 = jnp.bfloat16

NX, NY, NZ, MX, MY, MZ, C = 128, 64, 128, 32, 16, 16, 32
GX, DP = 32, 8
SLAB = NX // GX
GRID_SCALE = 1.0 / math.sqrt(NX * NY * NZ)
MODE_SCALE = 1.0 / math.sqrt(MX * MY * MZ)
PIECE = (GX, 16, 128)
ROUNDS = (0, 1, 2, 3)


def angles(length, freqs):
    phase = (np.arange(length)[:, None] * freqs[None, :]) % length
    angle = np.float32(2.0 * math.pi / length) * phase.astype(np.float32)
    return np.cos(angle).astype(np.float32), np.sin(angle).astype(np.float32)


def signed(count):
    k = np.arange(count)
    return np.where(k < count // 2, k, k - count)


def tables():
    bf = ml_dtypes.bfloat16
    cz, sz = angles(NZ, np.arange(MZ))
    zt = np.zeros((MZ, 2, 8, 8, NZ), np.float32)
    for q in range(8):
        zt[:, 0, q, q, :] = cz.T
        zt[:, 1, q, q, :] = -sz.T
    cy, sy = angles(NY, signed(MY))
    yb = np.stack([cy, -sy], axis=1)
    lt = np.einsum("ybk,cd->ycbkd", yb, np.eye(16, dtype=np.float32))
    cx, sx = angles(NX, signed(MX))
    rot = np.stack([np.stack([cx, sx]), np.stack([-sx, cx])])
    rot = rot.reshape(2, 2, GX, SLAB, MX)
    xf = np.einsum("pagrk,hj->phkgajr", rot, np.eye(2, dtype=np.float32))
    xf = xf.reshape(128, 512)
    return (
        zt.reshape(256, 1024).astype(bf),
        np.ascontiguousarray(zt.reshape(256, 1024).T).astype(bf),
        lt.reshape(1024, 512).astype(bf),
        xf.astype(bf),
        np.ascontiguousarray(xf.T).astype(bf),
    )


def dot(a, b):
    return jnp.dot(a, b, preferred_element_type=F32)


def dot_nt(a, b):
    return lax.dot_general(a, b, (((1,), (1,)), ((), ())), preferred_element_type=F32)


def iota(shape, axis):
    return lax.broadcasted_iota(jnp.int32, shape, axis)


def swap16(x):
    _, rows, _ = x.shape
    for s in (1, 2, 4, 8):
        keep_low = (iota((rows, 128), 1) & s) == 0
        parts = [None] * 16
        for i in range(16):
            if i & s:
                continue
            low, high = x[i], x[i + s]
            parts[i] = jnp.where(keep_low, low, pltpu.roll(high, s, 1))
            parts[i + s] = jnp.where(keep_low, pltpu.roll(low, 128 - s, 1), high)
        x = parts if s == 8 else _Stack(parts, rows)
    return x


class _Stack:
    def __init__(self, parts, rows):
        self.parts, self.shape = parts, (16, rows, 128)

    def __getitem__(self, i):
        return self.parts[i]


def gelu_pair(x):
    k0 = math.sqrt(2.0 / math.pi)
    u = x * (k0 + (k0 * 0.044715) * (x * x))
    t = jnp.tanh(u)
    half = 0.5 * t + 0.5
    slope = half + (1.5 * u - k0 * x) * (1.0 - t * t)
    return x * half, slope


def kernel(
    x_hbm, w_hbm, s_hbm, ct_hbm, zt_hbm, zf_hbm, lt_hbm, xf_hbm, xi_hbm,
    out_hbm, gin_hbm, wg_hbm,
    f_v, ct_v, o_v, gp_v, zt_v, zf_v, lt_v, xf_v, xi_v, wl_v,
    sw, sa1, sd1, sa2, sd2, swg,
    ra1, rd1, ra2, rd2, rwg,
    wall, mall, ball,
    m_v, p_v, q_v, gx_v, e_v, sk_v, t_v, sk_w, wt_v, ks_v, kb_v,
    lsem, ss, rs,
):
    me = lax.axis_index("gx")
    d = lax.axis_index("dp")
    bar = pltpu.get_barrier_semaphore()

    def peer(q):
        i, j = q // 4, lax.rem(q, 4)
        dz = 4 + (1 - 2 * lax.rem(i, 2)) * ((i + 1) // 2)
        dy = 2 + (1 - 2 * lax.rem(j, 2)) * ((j + 1) // 2)
        return lax.rem(me // 4 + dz, 8) * 4 + lax.rem(lax.rem(me, 4) + dy, 4)

    def greet_g(q, c):
        pl.semaphore_signal(bar, inc=1, device_id={"gx": peer(q)}, device_id_type=MESH)
        return c

    def greet_d(p, c):
        pl.semaphore_signal(bar, inc=1, device_id={"dp": lax.rem(d + p, DP)}, device_id_type=MESH)
        return c

    pending = {}

    def load(name, src, dst, n):
        copy = pltpu.make_async_copy(src, dst, lsem.at[n])
        copy.start()
        pending[name] = copy.wait

    def settle(*names):
        for name in names:
            pending.pop(name)()

    def wait_bytes(ref, sem, count):
        view = ref.at[pl.ds(0, count)]
        pltpu.make_async_copy(view, view, sem).wait()

    def expect(name, n, ref, count):
        pending[name] = lambda: wait_bytes(ref, rs.at[n], count)
        pending[name + "_sent"] = lambda: wait_bytes(ref, ss.at[n], count)

    part, ih0, oh0 = d // 4, lax.rem(d // 2, 2), lax.rem(d, 2)
    w_mine = w_hbm.at[part, pl.ds(ih0 * 16, 16), pl.ds(oh0 * 16, 16), :]
    load("w", w_mine, wl_v, 0)
    lax.fori_loop(0, GX - 1, greet_g, 0, unroll=True)
    lax.fori_loop(1, DP, greet_d, 0, unroll=True)
    load("zf", zf_hbm, zf_v, 1)
    load("f", x_hbm, f_v, 2)
    load("lt", lt_hbm, lt_v, 3)
    load("s", s_hbm, sk_w, 11)
    load("xf", xf_hbm, xf_v, 4)
    load("xi", xi_hbm, xi_v, 5)
    load("zt", zt_hbm, zt_v, 10)
    load("ct", ct_hbm, ct_v, 6)

    def spread(name, send, recv, n):
        def body(q, c):
            t = peer(q)
            pltpu.make_async_remote_copy(
                send.at[t], recv.at[me], ss.at[n], rs.at[n],
                device_id={"gx": t}, device_id_type=MESH,
            ).start()
            return c

        lax.fori_loop(0, GX - 1, body, 0, unroll=True)
        recv[me] = send[me]
        expect(name, n, recv, GX - 1)

    def share(name, buf, n):
        def body(p, c):
            pltpu.make_async_remote_copy(
                buf.at[d], buf.at[d], ss.at[n], rs.at[n],
                device_id={"dp": lax.rem(d + p, DP)}, device_id_type=MESH,
            ).start()
            return c

        for p in (4, 5, 3, 6, 2, 7, 1):
            body(p, 0)
        expect(name, n, buf, DP - 1)

    settle("w")
    for kyh in range(2):
        swapped = swap16(wl_v[:, :, kyh * 128:(kyh + 1) * 128].astype(F32))
        for kz in range(16):
            sw[kyh * 16 + kz] = swapped[kz].astype(BF16)

    def planes(field, send):
        for t in range(4):
            blocks = [
                field[x, pl.ds(t * 16, 16), h].reshape(256, 128)
                for h in range(2) for x in range(SLAB)
            ]
            along_z = dot(jnp.concatenate(blocks, axis=1), zf_v[...])
            t_v[:, t * 256:(t + 1) * 256] = along_z.T.astype(BF16)
        u = dot(t_v[...], lt_v[...])
        u = u.reshape(16, 2, 8, 512)
        u0, u1 = u[:, 0], u[:, 1]
        re = u0[:, :, :256] - u1[:, :, 256:]
        im = u0[:, :, 256:] + u1[:, :, :256]
        both = jnp.stack([re, im], axis=1).reshape(16, 16, 256).astype(BF16)
        send[0:16] = both[:, :, :128]
        send[16:32] = both[:, :, 128:]

    pl.semaphore_wait(bar, GX - 1 + DP - 1)

    def body_w(q, c):
        t = peer(q)
        pltpu.make_async_remote_copy(
            sw.at[t], wall.at[d, q], ss.at[0], rs.at[20 + q // 8],
            device_id={"gx": t}, device_id_type=MESH,
        ).start()
        return c

    for r in ROUNDS:
        lax.fori_loop(8 * r, min(8 * r + 8, GX - 1), body_w, 0, unroll=True)
    wall[d, GX - 1] = sw[me]
    pending["weights_sent"] = lambda: wait_bytes(sw, ss.at[0], GX - 1)
    for r in ROUNDS:
        pending[f"weights_gx{r}"] = lambda r=r: wait_bytes(sw, rs.at[20 + r], min(8, GX - 1 - 8 * r))
    settle("zf", "lt", "f")
    planes(f_v, sa1)
    spread("a1", sa1, ra1, 1)

    er = iota((256, 32), 0)
    expand = (lax.rem(er, 32) == iota((256, 32), 1)).astype(F32).astype(BF16)
    same = iota((256, 256), 0) // 32 == iota((256, 256), 1) // 32
    settle("s")
    sk = sk_w[...]
    es = dot(expand, sk).astype(BF16)
    kb_v[...] = jnp.where(same, dot_nt(es, expand), 0.0).astype(BF16)
    est = dot_nt(expand, sk).astype(BF16)
    ks_v[...] = jnp.where(same, dot_nt(est, expand), 0.0).astype(BF16)
    sum_l = (iota((64, 1024), 0) == iota((64, 1024), 1) // 16).astype(F32).astype(BF16)
    rep_l = (iota((1024, 64), 0) // 16 == iota((1024, 64), 1)).astype(F32).astype(BF16)
    ones_b = (iota((128, 128), 0) // 16 == iota((128, 128), 1) // 16).astype(F32).astype(BF16)
    diag = lax.rem(iota((1024, 128), 0), 16) == lax.rem(iota((1024, 128), 1), 16)


    mate = d + 1 - 2 * lax.rem(d, 2)

    def gather(s, r, target, send_n, recv_n):
        block = wall.at[s, pl.ds(8 * r, 8)]
        pltpu.make_async_remote_copy(
            block, block, ss.at[send_n], rs.at[recv_n],
            device_id={"dp": target}, device_id_type=MESH,
        ).start()

    def source(q):
        i, j = q // 4, lax.rem(q, 4)
        dz = 4 + (1 - 2 * lax.rem(i, 2)) * ((i + 1) // 2)
        dy = 2 + (1 - 2 * lax.rem(j, 2)) * ((j + 1) // 2)
        return lax.rem(me // 4 + 8 - dz, 8) * 4 + lax.rem(lax.rem(me, 4) + 4 - dy, 4)

    for r in ROUNDS:
        settle(f"weights_gx{r}")
        for p in (2, 1, 3):
            gather(d, r, lax.rem(d + 2 * p, DP), 2, 24 + 3 * r + p - 1)
        gather(d, r, mate, 3, 36 + r)

    for r in ROUNDS:
        for p in (1, 3, 2):
            pending[f"weights_x{r}{p}"] = lambda n=24 + 3 * r + p - 1: wait_bytes(wall.at[0], rs.at[n], 8)
        pending[f"weights_core{r}"] = lambda r=r: wait_bytes(wall.at[0], rs.at[36 + r], GX)
    pending["weights_x_sent"] = lambda: wait_bytes(wall, ss.at[2], 3)
    pending["weights_core_sent"] = lambda: wait_bytes(wall, ss.at[3], 4)
    for r in ROUNDS:
        for p in (1, 3, 2):
            settle(f"weights_x{r}{p}")
            gather(lax.rem(d + 8 - 2 * p, DP), r, mate, 3, 36 + r)

    def to_modes(recv, scale):
        r = recv[...].reshape(512, 128)
        return (dot(xf_v[...], r) * scale).astype(BF16)

    def to_slabs(mixed, send):
        send[...] = dot(xi_v[...], mixed).astype(BF16).reshape(PIECE)

    settle("xf", "xi", "a1")
    modes = to_modes(ra1, GRID_SCALE)
    mall[d] = modes
    m_v[...] = modes.astype(F32)


    def weight(a, h, oh, q):
        return wall[4 * a + 2 * h + oh, q].astype(F32)

    def mix(q, c):
        k = source(q)
        mr = [m_v[pl.ds(h * 32 + k, 1), :] for h in range(2)]
        mi = [m_v[pl.ds(64 + h * 32 + k, 1), :] for h in range(2)]
        for oh in range(2):
            re = im = None
            for h in range(2):
                wr, wi = weight(0, h, oh, q), weight(1, h, oh, q)
                r = wr * mr[h] - wi * mi[h]
                i = wr * mi[h] + wi * mr[h]
                re = r if re is None else re + r
                im = i if im is None else im + i
            row = pl.multiple_of(oh * 512 + k * 16, 16)
            p_v[0, pl.ds(row, 16), :] = re.astype(BF16)
            p_v[1, pl.ds(row, 16), :] = im.astype(BF16)
        return c

    for r in ROUNDS:
        settle(f"weights_core{r}")
        lax.fori_loop(8 * r, 8 * r + 8, mix, 0, unroll=True)
    mixed = []
    for a in range(2):
        q = jnp.where(diag, dot(p_v[a], ones_b), 0.0).astype(BF16)
        mixed.append(dot(sum_l, q))
    to_slabs(jnp.concatenate(mixed, axis=0).astype(BF16), sd1)
    spread("d1", sd1, rd1, 5)

    def unpack(recv):
        g = recv[...].astype(F32)
        g = jnp.concatenate([g[:16], g[16:]], axis=2).reshape(16, 2, 8, 256)
        turned = jnp.stack([g[:, 1], -g[:, 0]], axis=1).reshape(256, 256)
        gx_v[0:256, :] = g.reshape(256, 256).T.astype(BF16)
        gx_v[256:512, :] = turned.T.astype(BF16)

    def skips(source, channel_map):
        for t in range(8):
            rows = slice(t * 8, t * 8 + 8)
            src = jnp.concatenate(
                [source[x, rows].reshape(256, 128) for x in range(SLAB)], axis=1
            )
            skip = dot(channel_map[...], src).reshape(8, 2, 16, 512)
            for x in range(SLAB):
                sk_v[x, rows] = skip[..., x * 128:(x + 1) * 128]

    def fields(scale, emit):
        for t in range(4):
            vt = (dot(lt_v[t * 256:(t + 1) * 256, :], gx_v[...]) * scale).astype(BF16)
            for x in range(0, SLAB, 2):
                for h in range(2):
                    lo = (h * 4 + x) * 128
                    fld = dot(vt, zt_v[:, lo:lo + 256]).reshape(16, 16, 256)
                    for i in range(2):
                        rows = pl.ds(t * 16, 16)
                        total = fld[:, :, i * 128:(i + 1) * 128] + sk_v[x + i, rows, h]
                        emit(x + i, rows, h, total)

    share("mall", mall, 4)
    skips(f_v, ks_v)
    settle("ct", "zt", "d1")
    unpack(rd1)

    def emit_forward(x, rows, h, pre):
        act, slope = gelu_pair(pre)
        o_v[x, rows, h] = act.astype(BF16)
        gp_v[x, rows, h] = (ct_v[x, rows, h].astype(F32) * slope).astype(BF16)

    fields(MODE_SCALE, emit_forward)
    load("out", o_v, out_hbm, 7)

    planes(gp_v, sa2)
    spread("a2", sa2, ra2, 6)
    skips(gp_v, kb_v)
    settle("a2")
    back = to_modes(ra2, MODE_SCALE)
    ball[d] = back
    share("ball", ball, 7)

    for a in range(2):
        rows = jnp.where(diag, dot(rep_l, back[64 * a:64 * a + 64]), 0.0).astype(BF16)
        q_v[a] = dot(rows, ones_b)

    def conj_mix(q, c):
        k = source(q)
        for h in range(2):
            re = im = None
            for oh in range(2):
                row = pl.multiple_of(oh * 512 + k * 16, 16)
                br, bi = q_v[0, pl.ds(row, 16), :], q_v[1, pl.ds(row, 16), :]
                wr, wi = weight(0, h, oh, q), weight(1, h, oh, q)
                r = wr * br + wi * bi
                i = wr * bi - wi * br
                re = r if re is None else re + r
                im = i if im is None else im + i
            row = pl.multiple_of(h * 512 + k * 16, 16)
            p_v[0, pl.ds(row, 16), :] = re.astype(BF16)
            p_v[1, pl.ds(row, 16), :] = im.astype(BF16)
        return c

    lax.fori_loop(0, MX, conj_mix, 0, unroll=16)
    back_modes = [dot(sum_l, p_v[a]) for a in range(2)]
    to_slabs(jnp.concatenate(back_modes, axis=0).astype(BF16), sd2)
    spread("d2", sd2, rd2, 8)

    settle("mall")
    sel_r, sel_c = iota((128, 512), 0), iota((128, 512), 1)
    chan = 4 * lax.rem(d, 4) + sel_c // 128
    pick = (lax.rem(sel_r, 16) == chan) & (sel_r // 16 == lax.rem(sel_c, 128) // 16)
    pick = pick.astype(F32).astype(BF16)
    ihd = d // 4
    for a in range(2):
        start = pl.multiple_of(a * 64 + ihd * 32, 32)
        rows = mall[:, pl.ds(start, 32), :].reshape(256, 128)
        e_v[a] = dot(rows, pick)
    settle("ball")
    for oh in range(2):
        for i4 in range(4):
            def add(n, acc):
                re, im = acc
                row = pl.multiple_of(n * 32, 32)
                er_ = e_v[0, pl.ds(row, 32), i4 * 128:(i4 + 1) * 128]
                ei_ = e_v[1, pl.ds(row, 32), i4 * 128:(i4 + 1) * 128]
                br = ball[n, oh * 32:oh * 32 + 32, :].astype(F32)
                bi = ball[n, 64 + oh * 32:64 + oh * 32 + 32, :].astype(F32)
                return re + er_ * br + ei_ * bi, im + er_ * bi - ei_ * br

            zero = jnp.zeros((32, 128), F32)
            re, im = lax.fori_loop(0, DP, add, (zero, zero), unroll=True)
            wt_v[:, i4 * 2 + oh, :] = re
            wt_v[:, 8 + i4 * 2 + oh, :] = im
    swg[...] = wt_v[...].astype(BF16)
    spread("wg", swg, rwg, 9)

    settle("d2", "out")
    unpack(rd2)

    def emit_backward(x, rows, h, total):
        o_v[x, rows, h] = total.astype(BF16)

    fields(GRID_SCALE, emit_backward)
    load("gin", o_v, gin_hbm, 8)

    settle("wg")
    load("wg_out", rwg, wg_hbm, 9)
    settle(*list(pending))


def writer(out_a, gin_a, wg_a, out_b, gin_b, wg_b, pieces, wo_v, sem):
    first = pltpu.make_async_copy(wg_a, pieces, sem.at[9])
    first.start()
    pairs = [(a.at[i], b.at[i]) for a, b in ((out_a, out_b), (gin_a, gin_b)) for i in range(SLAB)]
    copies = [pltpu.make_async_copy(a, b, sem.at[n]) for n, (a, b) in enumerate(pairs)]
    for copy in copies:
        copy.start()
    first.wait()
    for kyh in range(2):
        swapped = swap16(pieces[kyh * 16:kyh * 16 + 16].astype(F32))
        for o in range(16):
            wo_v[:, o, kyh * 128:(kyh + 1) * 128] = swapped[o]
    last = pltpu.make_async_copy(wo_v, wg_b, sem.at[8])
    last.start()
    for copy in copies:
        copy.wait()
    last.wait()


def per_device(inputs, spectral_weights, skip_weights, cotangent, *tabs):
    shape5 = (SLAB, NY, 2, 16, NZ)
    any_spec = pl.BlockSpec(memory_space=pl.ANY)
    vm = pltpu.VMEM
    big = vm(shape5, BF16)
    piece = vm(PIECE, BF16)
    hbm = pl.BlockSpec(memory_space=pltpu.HBM)
    keep = functools.partial(pltpu.with_memory_space_constraint, memory_space=pltpu.HBM)
    shapes = [
        jax.ShapeDtypeStruct(shape5, BF16),
        jax.ShapeDtypeStruct(shape5, BF16),
        jax.ShapeDtypeStruct((16, 16, 256), F32),
    ]
    results = pl.pallas_call(
        kernel,
        out_shape=[vm(shape5, BF16), vm(shape5, BF16), piece],
        in_specs=[hbm] * 9,
        out_specs=[any_spec] * 3,
        scratch_shapes=[
            big, big, big, big,
            vm((256, 1024), BF16), vm((1024, 256), BF16), vm((1024, 512), BF16),
            vm((128, 512), BF16), vm((512, 128), BF16),
            vm((16, 16, 256), BF16),
            *([piece] * 11),
            vm((DP, *PIECE), BF16), vm((DP, 128, 128), BF16), vm((DP, 128, 128), BF16),
            vm((128, 128), F32), vm((2, 1024, 128), BF16), vm((2, 1024, 128), F32),
            vm((512, 256), BF16), vm((2, 256, 512), F32), vm(shape5, F32), vm((256, 1024), BF16), vm((32, 32), BF16),
            vm(PIECE, F32),
            vm((256, 256), BF16), vm((256, 256), BF16),
            *([pltpu.SemaphoreType.DMA((40,))] * 3),
        ],
        compiler_params=pltpu.CompilerParams(
            collective_id=0, has_side_effects=True, vmem_limit_bytes=40 * 1024 * 1024
        ),
        cost_estimate=pl.CostEstimate(flops=8_000_000_000, bytes_accessed=12_000_000, transcendentals=1_048_576),
        name="spectral_layer",
    )(
        keep(inputs.reshape(shape5)), keep(spectral_weights[0]), keep(skip_weights),
        keep(cotangent.reshape(shape5)), *map(keep, tabs),
    )
    out, gin, wg = pl.pallas_call(
        writer,
        out_shape=shapes,
        in_specs=[any_spec] * 3,
        out_specs=[hbm] * 3,
        scratch_shapes=[piece, vm((16, 16, 256), F32), pltpu.SemaphoreType.DMA((10,))],
        compiler_params=pltpu.CompilerParams(vmem_limit_bytes=4 * 1024 * 1024),
        name="write_results",
    )(*results)
    return (
        out.reshape(inputs.shape),
        gin.reshape(inputs.shape),
        wg.reshape(1, 2, 4, C, MY * MZ),
    )


def solution(mesh):
    field_spec = P("dp", "gx", None, None, None)
    in_specs = (field_spec, P("gx", None, None, None, None), P(), field_spec) + (P(),) * 5
    out_specs = (field_spec, field_spec, P("gx", None, "dp", None, None))
    mapped = jax.shard_map(
        per_device, mesh=mesh, in_specs=in_specs, out_specs=out_specs, check_vma=False
    )
    tabs = tables()

    def run(inputs, spectral_weights, skip_weights, cotangent):
        return mapped(
            inputs, spectral_weights, skip_weights, cotangent, *[jnp.asarray(t) for t in tabs]
        )

    return run
```
